32 devices in a mesh: parts: 2 (over y), row: 8 (over z, x), rep: 2 (over core).
Axes of the slice: x: 2, y: 2, z: 4, core: 2. Of those that a mesh axis runs over, the one named last changes fastest.
Arguments:
- features: bfloat16 [4096, 128], P(('parts', 'row')), parts along dimension 0, may hold values from -6 to 6
- tile_values: bfloat16 [16384, 4096], P(('parts', 'row', 'rep')), parts along dimension 0, may hold values from 0 to 1, as said below
- tile_cols: int32 [16384], P(('parts', 'row', 'rep')), parts along dimension 0, may hold values from 0 to 31, as said below
- tile_rows: int32 [16384], P(('parts', 'row', 'rep')), parts along dimension 0, may hold values from 0 to 1
- tile_count: int32 [32], P(('parts', 'row', 'rep')), parts along dimension 0, may hold values from 128 to 512, as said below
- labels: int32 [4096], P(('parts', 'row', 'rep')), parts along dimension 0, may hold values from 0 to 171
- w_self: bfloat16 [128, 256], replicated, may hold values from -0.5 to 0.5
- w_neigh: bfloat16 [128, 256], replicated, may hold values from -0.5 to 0.5
- w_out: bfloat16 [256, 172], replicated
Outputs:
- hidden: bfloat16 [4096, 256], P(('parts', 'row', 'rep')), parts along dimension 0
- grad_self: float32 [256, 256], P(('parts', 'rep')), parts along dimension 0
- grad_neigh: float32 [256, 256], P(('parts', 'rep')), parts along dimension 0
- grad_out: float32 [512, 172], P(('parts', 'rep')), parts along dimension 0
The draws below stay inside these ranges and needn't reach their ends.
There are 2 independent parts, one for each index of `parts`. The reference program is written for one: setup_inputs(seed, part) draws one part's arguments, and reference() takes and returns one part's arrays. A program takes and returns all parts, laid end to end along the dimension named above; an argument that names none is the same for every part. Nothing has to cross between parts.
Inputs may be any that keep to these rules, and one draw needn't show every extreme that they name: `tile_cols`: slot t < 2 of device d is its own diagonal tile: destination tile t, source tile d * 2 + t. Other slots may repeat places. `tile_count`: live slots come first in a device's list; some device has all 512 live. `tile_values`: most entries of a tile are zero; every nonzero is at least 0.05. The diagonal entries of a device's own diagonal tiles are nonzero.
All inputs are finite; a program needn't handle non-finite values.
Results may differ from the reference program's by a relative error of at most 0.001.
The reference program's roundings to bfloat16 on the way (of `neigh`, `d_logits` and `d_pre`) count: a program that leaves them out, or rounds other values in their place, can miss the bound.
Values may be sent and summed in bfloat16 or wider, within the bound.
A program may use at most 64 MiB of HBM per device.

```python
import math
import jax
import jax.numpy as jnp
from jax import lax

F = 128
HID = 256
C = 172
TB = 64
ROWS_DEV = 128
TCAP = 512
NODES = 2048
TILES = 8192
N_ROW = 8
N_REP = 2


def draw_tile_values(key, part):
    key = jax.random.fold_in(key, 15)
    key_a, key_b = jax.random.split(key, 2)
    dst_tiles = ROWS_DEV // TB
    position = (jnp.arange(TILES) % TCAP)[:, None]
    entry = jnp.arange(TB * TB)[None, :]
    on_diag = entry // TB == entry % TB
    diag_slot = position < dst_tiles
    spread = jax.random.uniform(key_a, (TILES, TB * TB), jnp.float32, math.log(0.05), 0.0)
    magnitude = jnp.exp(spread)
    roll = jax.random.randint(key_b, (TILES, TB * TB), 0, 2 * TB)
    keep = jnp.where(diag_slot, roll < TB // 4, roll < 1) | diag_slot & on_diag
    return jnp.where(keep, magnitude, 0.0).astype(jnp.bfloat16)


def draw_tile_cols(key, part):
    key = jax.random.fold_in(key, 11)
    dst_tiles = ROWS_DEV // TB
    tile_total = NODES // TB
    slot = jnp.arange(TILES)
    owner = slot // TCAP
    position = slot % TCAP
    key_a, key_b, key_c, key_d = jax.random.split(key, 4)
    spread = jax.random.randint(key_a, (TILES,), 0, tile_total)
    hubs = jax.random.randint(key_b, (16,), 0, tile_total)
    pick = jax.random.randint(key_c, (TILES,), 0, 16)
    use_hub = jax.random.randint(key_d, (TILES,), 0, 4) == 0
    chosen = jnp.where(use_hub, hubs[pick], spread)
    return jnp.where(position < dst_tiles, owner * dst_tiles + position, chosen).astype(jnp.int32)


def draw_tile_rows(key, part):
    key = jax.random.fold_in(key, 12)
    dst_tiles = ROWS_DEV // TB
    position = jnp.arange(TILES) % TCAP
    drawn = jax.random.randint(key, (TILES,), 0, dst_tiles)
    return jnp.where(position < dst_tiles, position, drawn).astype(jnp.int32)


def draw_tile_count(key, part):
    key = jax.random.fold_in(key, 13)
    devices = N_ROW * N_REP
    key_a, key_b, key_c = jax.random.split(key, 3)
    counts = jax.random.randint(key_a, (devices,), TCAP // 4, TCAP + 1)
    fullest = jax.random.randint(key_b, (), 0, devices)
    emptiest = (fullest + 1 + jax.random.randint(key_c, (), 0, devices - 1)) % devices
    index = jnp.arange(devices)
    counts = jnp.where(index == fullest, TCAP, counts)
    counts = jnp.where(index == emptiest, TCAP // 4, counts)
    return counts.astype(jnp.int32)


def draw_w_out(key, part):
    key = jax.random.fold_in(key, 14)
    weights = jax.random.normal(key, (HID, C), jnp.float32) / jnp.sqrt(jnp.float32(HID))
    return weights.astype(jnp.bfloat16)


def plant(result, rng, least, high):
    shape = result.shape
    index_at = [jax.random.randint(jax.random.fold_in(rng, axis), (), 0, shape[axis]) for axis in range(len(shape))]
    result = result.at[tuple(index_at)].set(least)
    longest = shape.index(max(shape))
    index_at[longest] = (index_at[longest] + 1) % shape[longest]
    return result.at[tuple(index_at)].set(high)


def steps_of(rng, dims, cuts, least, largest):
    gain, own = 1.0, jax.random.fold_in(rng, 6)
    for dim, shards_of in cuts:
        heights = jnp.exp(jax.random.uniform(jax.random.fold_in(own, dim), (shards_of,), jnp.float32, least / len(cuts), largest / len(cuts)))
        gain = gain * jnp.repeat(heights, dims[dim] // shards_of).reshape([-1 if axis == dim else 1 for axis in range(len(dims))])
    return gain


def gaussian(rng, shape, width, reach, cuts=(), dtype=jnp.bfloat16):
    values = width * jax.random.normal(rng, shape, jnp.float32)
    if cuts:
        values = values * steps_of(rng, shape, cuts, -0.22, 0.18)
    return jnp.clip(values, -reach, reach).astype(dtype)


def setup_inputs(seed: int = 0, part: int = 0) -> dict:
    streams_of = jax.random.split(jax.random.key(seed), 10)
    own_keys = jax.random.split(jax.random.fold_in(streams_of[9], part), 10)
    features = gaussian(own_keys[0], (NODES, F), 1.0, 6.0, ((0, 8),))
    tile_values = draw_tile_values(jax.random.fold_in(jax.random.fold_in(streams_of[9], part), 71), part)
    tile_cols = draw_tile_cols(jax.random.fold_in(jax.random.fold_in(streams_of[9], part), 71), part)
    tile_rows = draw_tile_rows(jax.random.fold_in(jax.random.fold_in(streams_of[9], part), 71), part)
    tile_count = draw_tile_count(jax.random.fold_in(jax.random.fold_in(streams_of[9], part), 71), part)
    labels = plant(jax.random.randint(own_keys[5], (NODES,), 0, C), jax.random.fold_in(own_keys[5], 1), 0, C - 1).astype(jnp.int32)
    w_self = gaussian(streams_of[6], (F, HID), F ** -0.5, 0.5)
    w_neigh = gaussian(streams_of[7], (F, HID), F ** -0.5, 0.5)
    w_out = draw_w_out(jax.random.fold_in(streams_of[9], 71), part)
    return {"features": features, "tile_values": tile_values, "tile_cols": tile_cols, "tile_rows": tile_rows, "tile_count": tile_count, "labels": labels, "w_self": w_self, "w_neigh": w_neigh, "w_out": w_out}


step_slots = 64

def aggregate(blocks_all, values, src_cols, dst_rows, live_count):
    slot_total = values.shape[0]
    dst_tiles = ROWS_DEV // TB
    is_live = jnp.arange(slot_total) < live_count
    chosen = ((dst_rows[:, None] == jnp.arange(dst_tiles)[None, :]) & is_live[:, None]).astype(jnp.float32)
    turns = slot_total // step_slots
    tile_set = values.reshape(turns, step_slots, TB, TB)
    col_sets = src_cols.reshape(turns, step_slots)
    sel_sets = chosen.reshape(turns, step_slots, dst_tiles)

    def one_block(carry, pieces):
        tile_blk, col_blk, sel_blk = pieces
        gathered = blocks_all[col_blk]
        product = jnp.einsum('sij,sjf->sif', tile_blk.astype(jnp.float32), gathered.astype(jnp.float32), precision=lax.Precision.HIGHEST)
        total = carry[0] + jnp.einsum('st,sif->tif', sel_blk, product, precision=lax.Precision.HIGHEST)
        row_sums = lax.optimization_barrier(jnp.sum(tile_blk.astype(jnp.float32), axis=2))
        degree = carry[1] + jnp.einsum('st,si->ti', sel_blk, row_sums, precision=lax.Precision.HIGHEST)
        return ((total, degree), None)
    start = (jnp.zeros((dst_tiles, TB, F), jnp.float32), jnp.zeros((dst_tiles, TB), jnp.float32))
    (total, degree), _ = lax.scan(one_block, start, (tile_set, col_sets, sel_sets))
    averaged = total / degree[:, :, None]
    return averaged.reshape(dst_tiles * TB, F).astype(jnp.bfloat16)

def reference(features, tile_values, tile_cols, tile_rows, tile_count, labels, w_self, w_neigh, w_out):
    devices = N_ROW * N_REP
    blocks_all = features.reshape(NODES // TB, TB, F)

    def per_device(pieces):
        values, src_cols, dst_rows, live_count = pieces
        return aggregate(blocks_all, values, src_cols, dst_rows, live_count)
    neigh = lax.map(per_device, (tile_values.reshape(devices, TCAP, TB * TB), tile_cols.reshape(devices, TCAP), tile_rows.reshape(devices, TCAP), tile_count))
    neigh = neigh.reshape(NODES, F)
    pre_act = jnp.dot(features, w_self, preferred_element_type=jnp.float32) + jnp.dot(neigh, w_neigh, preferred_element_type=jnp.float32)
    hidden = jnp.maximum(pre_act, 0.0).astype(jnp.bfloat16)
    logits = jnp.dot(hidden, w_out, preferred_element_type=jnp.float32)
    row_max = lax.optimization_barrier(jnp.max(logits, axis=1, keepdims=True))
    expo = jnp.exp(logits - row_max)
    probability = expo / lax.optimization_barrier(jnp.sum(expo, axis=1, keepdims=True))
    one_hot = (labels[:, None] == jnp.arange(C)[None, :]).astype(jnp.float32)
    factor = 1.0 / math.sqrt(NODES)
    d_logits = ((probability - one_hot) * factor).astype(jnp.bfloat16)
    grad_out = jnp.dot(hidden.T, d_logits, preferred_element_type=jnp.float32)
    back = jnp.dot(d_logits, w_out.T, preferred_element_type=jnp.float32)
    d_pre = jnp.where(pre_act > 0.0, back, 0.0).astype(jnp.bfloat16)
    grad_self = jnp.dot(features.T, d_pre, preferred_element_type=jnp.float32)
    grad_neigh = jnp.dot(neigh.T, d_pre, preferred_element_type=jnp.float32)
    return (hidden, grad_self, grad_neigh, grad_out)
```

```python
import functools
import math

import jax
import jax.numpy as jnp
from jax import lax
from jax.experimental import pallas as pl
from jax.experimental.pallas import tpu as pltpu
from jax.sharding import PartitionSpec as P

F = 128
HID = 256
C = 172
TB = 64
LANES = 128
CHUNKS = 4
MESH = pl.DeviceIdType.MESH


def split_rows(n_row):
    used = 2 * F // 2 * 2 + -(-C // 8) * 8
    each = -(-used // (8 * n_row)) * 8
    return each, each * n_row


def fused(
    n_row, feat, values, cols, rows, count, labels, w_self, w_neigh, w_out,
    hidden_out, gs_out, gn_out, go_out,
    vbuf, spread, lhs, whole, order, part, got, held, slots, total,
    v_sem, ga_send, ga_recv, gb_send, gb_recv, ra_send, ra_recv, rb_send, rb_recv, rc_send, rc_recv,
):
    me_part = lax.axis_index("parts")
    me_row = lax.axis_index("row")
    me_rep = lax.axis_index("rep")
    other = 1 - me_rep
    rows_dev = hidden_out.shape[0]
    dst_tiles = rows_dev // TB
    n_col = n_row * 2 * dst_tiles
    n_slot, tile_size = values.shape
    wide = tile_size // CHUNKS
    pairs = tile_size // LANES
    each = slots.shape[1]

    def peer(step):
        return lax.rem(me_row + step, n_row)

    def at(row, rep):
        return (me_part, row, rep)

    loads = [
        pltpu.make_async_copy(values.at[:, pl.ds(n * wide, wide)], vbuf.at[n], v_sem.at[n])
        for n in range(CHUNKS)
    ]
    for copy in loads:
        copy.start()

    barrier = pltpu.get_barrier_semaphore()
    pl.semaphore_signal(barrier, inc=1, device_id=at(me_row, other), device_id_type=MESH)
    for step in range(1, n_row):
        pl.semaphore_signal(barrier, inc=1, device_id=at(peer(step), me_rep), device_id_type=MESH)
    pl.semaphore_wait(barrier, n_row)

    mine = pl.ds(pl.multiple_of(me_rep * rows_dev, rows_dev), rows_dev)
    across, beside = [], []
    for step in range(1, n_row):
        here = pl.ds(pl.multiple_of(me_row * 2 * rows_dev + me_rep * rows_dev, rows_dev), rows_dev)
        across.append(
            pltpu.make_async_remote_copy(
                feat.at[mine, :], whole.at[here, :], ga_send.at[step - 1], ga_recv.at[step - 1],
                device_id=at(peer(step), me_rep), device_id_type=MESH,
            )
        )
        source = lax.rem(me_row - step + n_row, n_row)
        came = pl.ds(pl.multiple_of(source * 2 * rows_dev + me_rep * rows_dev, rows_dev), rows_dev)
        beside.append(
            pltpu.make_async_remote_copy(
                whole.at[came, :], whole.at[came, :], gb_send.at[step - 1], gb_recv.at[step - 1],
                device_id=at(me_row, other), device_id_type=MESH,
            )
        )
    for copy in across:
        copy.start()

    slot = lax.broadcasted_iota(jnp.int32, (1, n_slot), 1)
    place = jnp.where(slot < count[0], rows[...] * n_col + cols[...], -1)
    places = lax.broadcasted_iota(jnp.int32, (dst_tiles * n_col, n_slot), 0)
    pick = jnp.where(places == place, 1.0, 0.0).astype(jnp.bfloat16)
    per_chunk = pairs // CHUNKS
    for n in range(CHUNKS):
        loads[n].wait()
        block = jnp.dot(pick, vbuf[n], preferred_element_type=jnp.float32)
        for k in range(per_chunk):
            spread[pl.ds(n * per_chunk + k, dst_tiles * n_col, stride=pairs), :] = block[
                :, k * LANES : (k + 1) * LANES
            ]

    height = dst_tiles * pairs
    sums = jnp.zeros((height, LANES), jnp.float32)
    for c in range(n_col):
        piece = jnp.concatenate(
            [spread[pl.ds((t * n_col + c) * pairs, pairs), :] for t in range(dst_tiles)], axis=0
        )
        sums = sums + piece
        high = piece.astype(jnp.bfloat16)
        low = (piece - high.astype(jnp.float32)).astype(jnp.bfloat16)
        lhs[0:height, pl.ds(c * LANES, LANES)] = high
        lhs[height : 2 * height, pl.ds(c * LANES, LANES)] = low
    degree = (
        jnp.sum(sums[:, :TB], axis=1, keepdims=True),
        jnp.sum(sums[:, TB:], axis=1, keepdims=True),
    )

    own = feat[mine, :]
    pre_self = jnp.dot(own, w_self[...], preferred_element_type=jnp.float32)
    own_t = own.astype(jnp.float32).T.astype(jnp.bfloat16)
    class_at = lax.broadcasted_iota(jnp.int32, (C, rows_dev), 0)
    one_hot = jnp.where(class_at == labels[...], 1.0, 0.0).T

    zero = jnp.zeros((TB, F), jnp.bfloat16)

    def half(ref, start, row, rep):
        pieces = []
        for q in range(dst_tiles):
            x = ref[pl.ds(pl.multiple_of(start + q * TB, TB), TB), :]
            pieces.append(jnp.concatenate([x, zero], axis=1))
            pieces.append(jnp.concatenate([zero, x], axis=1))
        depth = dst_tiles * LANES
        left = lhs[:, pl.ds(pl.multiple_of((row * 2 + rep) * depth, depth), depth)]
        return jnp.dot(left, jnp.concatenate(pieces, axis=0), preferred_element_type=jnp.float32)

    acc = half(feat, 0, me_row, 0) + half(feat, rows_dev, me_row, 1)
    for step in range(1, n_row):
        across[step - 1].wait_recv()
        beside[step - 1].start()
        source = lax.rem(me_row - step + n_row, n_row)
        acc = acc + half(whole, source * 2 * rows_dev + me_rep * rows_dev, source, me_rep)
    for step in range(1, n_row):
        beside[step - 1].wait_recv()
        source = lax.rem(me_row - step + n_row, n_row)
        acc = acc + half(whole, source * 2 * rows_dev + other * rows_dev, source, other)
    agg = acc[:height] + acc[height:]
    for b in range(2):
        order[pl.ds(b, height, stride=2), :] = agg[:, b * F : (b + 1) * F] / degree[b]
    neigh_f = order[...].astype(jnp.bfloat16).astype(jnp.float32)
    neigh = neigh_f.astype(jnp.bfloat16)

    pre = pre_self + jnp.dot(neigh, w_neigh[...], preferred_element_type=jnp.float32)
    hidden = jnp.maximum(pre, 0.0).astype(jnp.bfloat16)
    hidden_out[...] = hidden
    logits = jnp.dot(hidden, w_out[...], preferred_element_type=jnp.float32)
    expo = jnp.exp(logits - jnp.max(logits, axis=1, keepdims=True))
    probability = expo / jnp.sum(expo, axis=1, keepdims=True)
    factor = 1.0 / math.sqrt(rows_dev * n_row * 2)
    d_logits = ((probability - one_hot) * factor).astype(jnp.bfloat16)

    def to_partner(n, first, size):
        span = pl.ds(first, size)
        return pltpu.make_async_remote_copy(
            part.at[other, span, :], got.at[span, :], ra_send.at[n], ra_recv.at[n],
            device_id=at(me_row, other), device_id_type=MESH,
        )

    n_feat = F // 2
    top = 4 * n_feat
    all_rows = part.shape[1]
    sent = [to_partner(0, top, all_rows - top), to_partner(1, 0, 2 * n_feat), to_partner(2, 2 * n_feat, 2 * n_feat)]
    out_t = jnp.dot(
        d_logits.astype(jnp.float32).T.astype(jnp.bfloat16), hidden, preferred_element_type=jnp.float32
    )
    for h in range(2):
        part[h, top + C // 8 * 8 : all_rows, :] = jnp.zeros((all_rows - top - C // 8 * 8, LANES), jnp.float32)
        part[h, top : top + C, :] = out_t[:, h * LANES : (h + 1) * LANES]
    sent[0].start()
    back = lax.dot_general(
        d_logits, w_out[...], (((1,), (1,)), ((), ())), preferred_element_type=jnp.float32
    )
    d_pre = jnp.where(pre > 0.0, back, 0.0).astype(jnp.bfloat16)
    for n, left in enumerate((own_t, neigh_f.T.astype(jnp.bfloat16))):
        grad = jnp.dot(left, d_pre, preferred_element_type=jnp.float32)
        for h in range(2):
            for b in range(2):
                part[h, pl.ds((2 * n + b) * n_feat, n_feat), :] = grad[
                    h * n_feat : (h + 1) * n_feat, b * LANES : (b + 1) * LANES
                ]
        sent[1 + n].start()

    spans = (pl.ds(top, all_rows - top), pl.ds(0, 2 * n_feat), pl.ds(2 * n_feat, 2 * n_feat))
    for n in range(3):
        sent[n].wait_recv()
        held[spans[n], :] = part[me_rep, spans[n], :] + got[spans[n], :]
    apart = []
    for step in range(1, n_row):
        span = pl.ds(pl.multiple_of(peer(step) * each, each), each)
        apart.append(
            pltpu.make_async_remote_copy(
                held.at[span, :], slots.at[step - 1], rb_send.at[step - 1], rb_recv.at[step - 1],
                device_id=at(peer(step), me_rep), device_id_type=MESH,
            )
        )
        apart[-1].start()
    own_span = pl.ds(pl.multiple_of(me_row * each, each), each)
    result = held[own_span, :]
    for step in range(1, n_row):
        apart[step - 1].wait_recv()
        result = result + slots[step - 1]
    total[own_span, :] = result
    spreads = []
    for step in range(1, n_row):
        spreads.append(
            pltpu.make_async_remote_copy(
                total.at[own_span, :], total.at[own_span, :], rc_send.at[step - 1], rc_recv.at[step - 1],
                device_id=at(peer(step), me_rep), device_id_type=MESH,
            )
        )
        spreads[-1].start()
    for step in range(1, n_row):
        source = lax.rem(me_row - step + n_row, n_row)
        span = pl.ds(pl.multiple_of(source * each, each), each)
        pltpu.make_async_remote_copy(
            total.at[span, :], total.at[span, :], rc_send.at[step - 1], rc_recv.at[step - 1],
            device_id=at(peer(step), me_rep), device_id_type=MESH,
        ).wait_recv()
    for n, out in enumerate((gs_out, gn_out)):
        for b in range(2):
            out[:, b * LANES : (b + 1) * LANES] = total[pl.ds((2 * n + b) * n_feat, n_feat), :]
    go_out[...] = total[top : top + C, :].T
    for copy in across + beside + sent + apart + spreads:
        copy.wait_send()


def local(features, tile_values, tile_cols, tile_rows, tile_count, labels, w_self, w_neigh, w_out):
    rows_dev = labels.shape[0]
    n_row = lax.axis_size("row")
    n_slot, tile_size = tile_values.shape
    dst_tiles = rows_dev // TB
    n_col = n_row * 2 * dst_tiles
    pairs = tile_size // LANES
    each, all_rows = split_rows(n_row)
    vmem = pl.BlockSpec(memory_space=pltpu.VMEM)
    dma = pltpu.SemaphoreType.DMA
    peers = max(n_row - 1, 1)
    return pl.pallas_call(
        functools.partial(fused, n_row),
        out_shape=(
            jax.ShapeDtypeStruct((rows_dev, HID), jnp.bfloat16),
            jax.ShapeDtypeStruct((F // 2, HID), jnp.float32),
            jax.ShapeDtypeStruct((F // 2, HID), jnp.float32),
            jax.ShapeDtypeStruct((HID // 2, C), jnp.float32),
        ),
        in_specs=[
            vmem, pl.BlockSpec(memory_space=pl.ANY), vmem, vmem,
            pl.BlockSpec(memory_space=pltpu.SMEM), vmem, vmem, vmem, vmem,
        ],
        out_specs=(vmem,) * 4,
        scratch_shapes=[
            pltpu.VMEM((CHUNKS, n_slot, tile_size // CHUNKS), jnp.bfloat16),
            pltpu.VMEM((dst_tiles * n_col * pairs, LANES), jnp.float32),
            pltpu.VMEM((2 * dst_tiles * pairs, n_col * LANES), jnp.bfloat16),
            pltpu.VMEM((n_row * 2 * rows_dev, F), jnp.bfloat16),
            pltpu.VMEM((rows_dev, F), jnp.float32),
            pltpu.VMEM((2, all_rows, LANES), jnp.float32),
            pltpu.VMEM((all_rows, LANES), jnp.float32),
            pltpu.VMEM((all_rows, LANES), jnp.float32),
            pltpu.VMEM((peers, each, LANES), jnp.float32),
            pltpu.VMEM((all_rows, LANES), jnp.float32),
            dma((CHUNKS,)), dma((peers,)), dma((peers,)), dma((peers,)), dma((peers,)),
            dma((3,)), dma((3,)), dma((peers,)), dma((peers,)), dma((peers,)), dma((peers,)),
        ],
        compiler_params=pltpu.CompilerParams(
            collective_id=0, has_side_effects=True, vmem_limit_bytes=40 * 2**20
        ),
    )(
        features, tile_values, tile_cols.reshape(1, n_slot), tile_rows.reshape(1, n_slot),
        tile_count, labels.reshape(1, rows_dev), w_self, w_neigh, w_out,
    )


step_slots = 64


def aggregate(blocks_all, values, src_cols, dst_rows, live_count, rows_dev):
    slot_total = values.shape[0]
    dst_tiles = rows_dev // TB
    is_live = jnp.arange(slot_total) < live_count
    chosen = ((dst_rows[:, None] == jnp.arange(dst_tiles)[None, :]) & is_live[:, None]).astype(
        jnp.float32
    )
    turns = slot_total // step_slots
    tile_set = values.reshape(turns, step_slots, TB, TB)
    col_sets = src_cols.reshape(turns, step_slots)
    sel_sets = chosen.reshape(turns, step_slots, dst_tiles)

    def one_block(carry, pieces):
        tile_blk, col_blk, sel_blk = pieces
        gathered = blocks_all[col_blk]
        product = jnp.einsum("sij,sjf->sif", tile_blk, gathered, preferred_element_type=jnp.float32)
        total = carry[0] + jnp.einsum(
            "st,sif->tif", sel_blk, product, precision=lax.Precision.HIGHEST
        )
        row_sums = jnp.sum(tile_blk.astype(jnp.float32), axis=2)
        degree = carry[1] + jnp.einsum(
            "st,si->ti", sel_blk, row_sums, precision=lax.Precision.HIGHEST
        )
        return ((total, degree), None)

    start = (jnp.zeros((dst_tiles, TB, F), jnp.float32), jnp.zeros((dst_tiles, TB), jnp.float32))
    (total, degree), _ = lax.scan(one_block, start, (tile_set, col_sets, sel_sets))
    averaged = total / degree[:, :, None]
    return averaged.reshape(dst_tiles * TB, F).astype(jnp.bfloat16)


def local_wide(features, tile_values, tile_cols, tile_rows, tile_count, labels, w_self, w_neigh, w_out):
    rows_dev = labels.shape[0]
    n_row = lax.axis_size("row")
    n_rep = lax.axis_size("rep")
    rep_index = lax.axis_index("rep")
    own_rows = lax.dynamic_slice_in_dim(features, rep_index * rows_dev, rows_dev, 0)
    whole = lax.all_gather(features, "row", axis=0, tiled=True)
    blocks_all = whole.reshape(whole.shape[0] // TB, TB, F)
    neigh = aggregate(blocks_all, tile_values, tile_cols, tile_rows, tile_count[0], rows_dev)
    pre_act = jnp.dot(own_rows, w_self, preferred_element_type=jnp.float32) + jnp.dot(
        neigh, w_neigh, preferred_element_type=jnp.float32
    )
    hidden = jnp.maximum(pre_act, 0.0).astype(jnp.bfloat16)
    logits = jnp.dot(hidden, w_out, preferred_element_type=jnp.float32)
    row_max = jnp.max(logits, axis=1, keepdims=True)
    expo = jnp.exp(logits - row_max)
    probability = expo / jnp.sum(expo, axis=1, keepdims=True)
    one_hot = (labels[:, None] == jnp.arange(C)[None, :]).astype(jnp.float32)
    factor = 1.0 / math.sqrt(rows_dev * n_row * n_rep)
    d_logits = ((probability - one_hot) * factor).astype(jnp.bfloat16)
    part_out = jnp.dot(hidden.T, d_logits, preferred_element_type=jnp.float32)
    back = jnp.dot(d_logits, w_out.T, preferred_element_type=jnp.float32)
    d_pre = jnp.where(pre_act > 0.0, back, 0.0).astype(jnp.bfloat16)
    part_self = jnp.dot(own_rows.T, d_pre, preferred_element_type=jnp.float32)
    part_neigh = jnp.dot(neigh.T, d_pre, preferred_element_type=jnp.float32)
    summed = lax.psum((part_self, part_neigh, part_out), ("row", "rep"))
    feat_rows = F // n_rep
    hid_rows = HID // n_rep
    grad_self = lax.dynamic_slice_in_dim(summed[0], rep_index * feat_rows, feat_rows, 0)
    grad_neigh = lax.dynamic_slice_in_dim(summed[1], rep_index * feat_rows, feat_rows, 0)
    grad_out = lax.dynamic_slice_in_dim(summed[2], rep_index * hid_rows, hid_rows, 0)
    return (hidden, grad_self, grad_neigh, grad_out)


def solution(mesh):
    placed = (
        P(("parts", "row"), None),
        P(("parts", "row", "rep"), None),
        P(("parts", "row", "rep")),
        P(("parts", "row", "rep")),
        P(("parts", "row", "rep")),
        P(("parts", "row", "rep")),
        P(),
        P(),
        P(),
    )
    return jax.shard_map(
        local if mesh.shape["row"] <= 16 else local_wide,
        mesh=mesh,
        in_specs=placed,
        out_specs=(
            P(("parts", "row", "rep"), None),
            P(("parts", "rep"), None),
            P(("parts", "rep"), None),
            P(("parts", "rep"), None),
        ),
        check_vma=False,
    )
```

```python
import functools
import math

import jax
import jax.numpy as jnp
from jax import lax
from jax.experimental import pallas as pl
from jax.experimental.pallas import tpu as pltpu
from jax.sharding import PartitionSpec as P

F = 128
HID = 256
C = 172
TB = 64
LANES = 128
CHUNKS = 4
MESH = pl.DeviceIdType.MESH


def split_rows(n_row):
    used = 2 * F // 2 * 2 + -(-C // 8) * 8
    each = -(-used // (8 * n_row)) * 8
    return each, each * n_row


def fused(
    n_row, feat_in, values, cols_in, rows_in, count, labels_in, w_self_in, w_neigh_in, w_out_in,
    hidden_out, total,
    feat, cols, rows, labels, w_self, w_neigh, w_out, in_sem, vbuf, spread, lhs, whole, order, part, got, held, slots,
    v_sem, ga_send, ga_recv, gb_send, gb_recv, ra_send, ra_recv, rb_send, rb_recv, rc_send, rc_recv,
):
    me_part = lax.axis_index("parts")
    me_row = lax.axis_index("row")
    me_rep = lax.axis_index("rep")
    other = 1 - me_rep
    rows_dev = hidden_out.shape[0]
    dst_tiles = rows_dev // TB
    n_col = n_row * 2 * dst_tiles
    n_slot, tile_size = values.shape
    wide = tile_size // CHUNKS
    pairs = tile_size // LANES
    each = slots.shape[1]

    def peer(step):
        return lax.rem(me_row + step, n_row)

    def at(row, rep):
        return (me_part, row, rep)

    loads = [
        pltpu.make_async_copy(values.at[:, pl.ds(n * wide, wide)], vbuf.at[n], v_sem.at[n])
        for n in range(CHUNKS)
    ]
    inputs = [
        pltpu.make_async_copy(source, target, in_sem.at[n])
        for n, (source, target) in enumerate((
            (feat_in, feat), (cols_in, cols), (rows_in, rows), (labels_in, labels),
            (w_self_in, w_self), (w_neigh_in, w_neigh), (w_out_in, w_out),
        ))
    ]
    for copy in inputs[:3] + loads + inputs[3:]:
        copy.start()

    barrier = pltpu.get_barrier_semaphore()
    pl.semaphore_signal(barrier, inc=1, device_id=at(me_row, other), device_id_type=MESH)
    for step in range(1, n_row):
        pl.semaphore_signal(barrier, inc=1, device_id=at(peer(step), me_rep), device_id_type=MESH)
    pl.semaphore_wait(barrier, n_row)

    mine = pl.ds(pl.multiple_of(me_rep * rows_dev, rows_dev), rows_dev)
    across, beside = [], []
    for step in range(1, n_row):
        here = pl.ds(pl.multiple_of(me_row * 2 * rows_dev + me_rep * rows_dev, rows_dev), rows_dev)
        across.append(
            pltpu.make_async_remote_copy(
                feat.at[mine, :], whole.at[here, :], ga_send.at[step - 1], ga_recv.at[step - 1],
                device_id=at(peer(step), me_rep), device_id_type=MESH,
            )
        )
        source = lax.rem(me_row - step + n_row, n_row)
        came = pl.ds(pl.multiple_of(source * 2 * rows_dev + me_rep * rows_dev, rows_dev), rows_dev)
        beside.append(
            pltpu.make_async_remote_copy(
                whole.at[came, :], whole.at[came, :], gb_send.at[step - 1], gb_recv.at[step - 1],
                device_id=at(me_row, other), device_id_type=MESH,
            )
        )
    inputs[0].wait()
    for copy in across:
        copy.start()

    inputs[1].wait()
    inputs[2].wait()
    slot = lax.broadcasted_iota(jnp.int32, (1, n_slot), 1)
    place = jnp.where(slot < count[0], rows[...] * n_col + cols[...], -1)
    places = lax.broadcasted_iota(jnp.int32, (dst_tiles * n_col, n_slot), 0)
    pick = jnp.where(places == place, 1.0, 0.0).astype(jnp.bfloat16)
    per_chunk = pairs // CHUNKS
    for n in range(CHUNKS):
        loads[n].wait()
        block = jnp.dot(pick, vbuf[n], preferred_element_type=jnp.float32)
        for k in range(per_chunk):
            spread[pl.ds(n * per_chunk + k, dst_tiles * n_col, stride=pairs), :] = block[
                :, k * LANES : (k + 1) * LANES
            ]

    height = dst_tiles * pairs
    sums = jnp.zeros((height, LANES), jnp.float32)
    for c in range(n_col):
        piece = jnp.concatenate(
            [spread[pl.ds((t * n_col + c) * pairs, pairs), :] for t in range(dst_tiles)], axis=0
        )
        sums = sums + piece
        high = piece.astype(jnp.bfloat16)
        low = (piece - high.astype(jnp.float32)).astype(jnp.bfloat16)
        lhs[0:height, pl.ds(c * LANES, LANES)] = high
        lhs[height : 2 * height, pl.ds(c * LANES, LANES)] = low
    degree = (
        jnp.sum(sums[:, :TB], axis=1, keepdims=True),
        jnp.sum(sums[:, TB:], axis=1, keepdims=True),
    )

    for copy in inputs[3:]:
        copy.wait()
    own = feat[mine, :]
    pre_self = jnp.dot(own, w_self[...], preferred_element_type=jnp.float32)
    own_t = own.astype(jnp.float32).T.astype(jnp.bfloat16)
    class_at = lax.broadcasted_iota(jnp.int32, (C, rows_dev), 0)
    one_hot = jnp.where(class_at == labels[...], 1.0, 0.0).T

    zero = jnp.zeros((TB, F), jnp.bfloat16)

    def half(ref, start, row, rep):
        pieces = []
        for q in range(dst_tiles):
            x = ref[pl.ds(pl.multiple_of(start + q * TB, TB), TB), :]
            pieces.append(jnp.concatenate([x, zero], axis=1))
            pieces.append(jnp.concatenate([zero, x], axis=1))
        depth = dst_tiles * LANES
        left = lhs[:, pl.ds(pl.multiple_of((row * 2 + rep) * depth, depth), depth)]
        return jnp.dot(left, jnp.concatenate(pieces, axis=0), preferred_element_type=jnp.float32)

    acc = half(feat, 0, me_row, 0) + half(feat, rows_dev, me_row, 1)
    for step in range(1, n_row):
        across[step - 1].wait_recv()
        beside[step - 1].start()
        source = lax.rem(me_row - step + n_row, n_row)
        acc = acc + half(whole, source * 2 * rows_dev + me_rep * rows_dev, source, me_rep)
    for step in range(1, n_row):
        beside[step - 1].wait_recv()
        source = lax.rem(me_row - step + n_row, n_row)
        acc = acc + half(whole, source * 2 * rows_dev + other * rows_dev, source, other)
    agg = acc[:height] + acc[height:]
    for b in range(2):
        order[pl.ds(b, height, stride=2), :] = agg[:, b * F : (b + 1) * F] / degree[b]
    neigh_f = order[...].astype(jnp.bfloat16).astype(jnp.float32)
    neigh = neigh_f.astype(jnp.bfloat16)

    pre = pre_self + jnp.dot(neigh, w_neigh[...], preferred_element_type=jnp.float32)
    hidden = jnp.maximum(pre, 0.0).astype(jnp.bfloat16)
    hidden_out[...] = hidden
    logits = lax.dot_general(
        hidden, w_out[...], (((1,), (1,)), ((), ())), preferred_element_type=jnp.float32
    )
    expo = jnp.exp(logits - jnp.max(logits, axis=1, keepdims=True))
    probability = expo / jnp.sum(expo, axis=1, keepdims=True)
    factor = 1.0 / math.sqrt(rows_dev * n_row * 2)
    d_logits = ((probability - one_hot) * factor).astype(jnp.bfloat16)

    def to_partner(n, first, size):
        span = pl.ds(first, size)
        return pltpu.make_async_remote_copy(
            part.at[other, span, :], got.at[span, :], ra_send.at[n], ra_recv.at[n],
            device_id=at(me_row, other), device_id_type=MESH,
        )

    n_feat = F // 2
    top = 4 * n_feat
    all_rows = part.shape[1]
    sent = [to_partner(0, top, all_rows - top), to_partner(1, 0, 2 * n_feat), to_partner(2, 2 * n_feat, 2 * n_feat)]
    out_t = jnp.dot(
        d_logits.astype(jnp.float32).T.astype(jnp.bfloat16), hidden, preferred_element_type=jnp.float32
    )
    for h in range(2):
        part[h, top + C // 8 * 8 : all_rows, :] = jnp.zeros((all_rows - top - C // 8 * 8, LANES), jnp.float32)
        part[h, top : top + C, :] = out_t[:, h * LANES : (h + 1) * LANES]
    sent[0].start()
    back = jnp.dot(d_logits, w_out[...], preferred_element_type=jnp.float32)
    d_pre = jnp.where(pre > 0.0, back, 0.0).astype(jnp.bfloat16)
    for n, left in enumerate((own_t, neigh_f.T.astype(jnp.bfloat16))):
        grad = jnp.dot(left, d_pre, preferred_element_type=jnp.float32)
        for h in range(2):
            for b in range(2):
                part[h, pl.ds((2 * n + b) * n_feat, n_feat), :] = grad[
                    h * n_feat : (h + 1) * n_feat, b * LANES : (b + 1) * LANES
                ]
        sent[1 + n].start()

    spans = (pl.ds(top, all_rows - top), pl.ds(0, 2 * n_feat), pl.ds(2 * n_feat, 2 * n_feat))
    for n in range(3):
        sent[n].wait_recv()
        held[spans[n], :] = part[me_rep, spans[n], :] + got[spans[n], :]
    apart = []
    for step in range(1, n_row):
        span = pl.ds(pl.multiple_of(peer(step) * each, each), each)
        apart.append(
            pltpu.make_async_remote_copy(
                held.at[span, :], slots.at[step - 1], rb_send.at[step - 1], rb_recv.at[step - 1],
                device_id=at(peer(step), me_rep), device_id_type=MESH,
            )
        )
        apart[-1].start()
    own_span = pl.ds(pl.multiple_of(me_row * each, each), each)
    result = held[own_span, :]
    for step in range(1, n_row):
        apart[step - 1].wait_recv()
        result = result + slots[step - 1]
    total[own_span, :] = result
    spreads = []
    for step in range(1, n_row):
        spreads.append(
            pltpu.make_async_remote_copy(
                total.at[own_span, :], total.at[own_span, :], rc_send.at[step - 1], rc_recv.at[step - 1],
                device_id=at(peer(step), me_rep), device_id_type=MESH,
            )
        )
        spreads[-1].start()
    for step in range(1, n_row):
        source = lax.rem(me_row - step + n_row, n_row)
        span = pl.ds(pl.multiple_of(source * each, each), each)
        pltpu.make_async_remote_copy(
            total.at[span, :], total.at[span, :], rc_send.at[step - 1], rc_recv.at[step - 1],
            device_id=at(peer(step), me_rep), device_id_type=MESH,
        ).wait_recv()
    for copy in across + beside + sent + apart + spreads:
        copy.wait_send()


def deliver(hidden, total, hidden_out, gs_out, gn_out, go_out, sem):
    n_feat = gs_out.shape[0]
    copies = [(hidden, hidden_out)]
    for n, out in enumerate((gs_out, gn_out)):
        for b in range(2):
            copies.append((
                total.at[pl.ds((2 * n + b) * n_feat, n_feat), :], out.at[:, pl.ds(b * LANES, LANES)]
            ))
    copies.append((total.at[pl.ds(4 * n_feat, C), :], go_out))
    moves = [pltpu.make_async_copy(a, b, sem.at[n]) for n, (a, b) in enumerate(copies)]
    for move in moves:
        move.start()
    for move in moves:
        move.wait()


def local(features, tile_values, tile_cols, tile_rows, tile_count, labels, w_self, w_neigh, w_out):
    rows_dev = labels.shape[0]
    n_row = lax.axis_size("row")
    n_slot, tile_size = tile_values.shape
    dst_tiles = rows_dev // TB
    n_col = n_row * 2 * dst_tiles
    pairs = tile_size // LANES
    each, all_rows = split_rows(n_row)
    vmem = pl.BlockSpec(memory_space=pltpu.VMEM)
    dma = pltpu.SemaphoreType.DMA
    peers = max(n_row - 1, 1)
    hbm = pl.BlockSpec(memory_space=pl.ANY)
    hidden, total = pl.pallas_call(
        functools.partial(fused, n_row),
        out_shape=(
            jax.ShapeDtypeStruct((rows_dev, HID), jnp.bfloat16),
            jax.ShapeDtypeStruct((all_rows, LANES), jnp.float32),
        ),
        in_specs=[hbm] * 4 + [pl.BlockSpec(memory_space=pltpu.SMEM)] + [hbm] * 4,
        out_specs=(vmem,) * 2,
        scratch_shapes=[
            pltpu.VMEM(features.shape, jnp.bfloat16),
            pltpu.VMEM((1, n_slot), jnp.int32),
            pltpu.VMEM((1, n_slot), jnp.int32),
            pltpu.VMEM((1, rows_dev), jnp.int32),
            pltpu.VMEM((F, HID), jnp.bfloat16),
            pltpu.VMEM((F, HID), jnp.bfloat16),
            pltpu.VMEM((C, HID), jnp.bfloat16),
            dma((7,)),
            pltpu.VMEM((CHUNKS, n_slot, tile_size // CHUNKS), jnp.bfloat16),
            pltpu.VMEM((dst_tiles * n_col * pairs, LANES), jnp.float32),
            pltpu.VMEM((2 * dst_tiles * pairs, n_col * LANES), jnp.bfloat16),
            pltpu.VMEM((n_row * 2 * rows_dev, F), jnp.bfloat16),
            pltpu.VMEM((rows_dev, F), jnp.float32),
            pltpu.VMEM((2, all_rows, LANES), jnp.float32),
            pltpu.VMEM((all_rows, LANES), jnp.float32),
            pltpu.VMEM((all_rows, LANES), jnp.float32),
            pltpu.VMEM((peers, each, LANES), jnp.float32),
            dma((CHUNKS,)), dma((peers,)), dma((peers,)), dma((peers,)), dma((peers,)),
            dma((3,)), dma((3,)), dma((peers,)), dma((peers,)), dma((peers,)), dma((peers,)),
        ],
        compiler_params=pltpu.CompilerParams(
            collective_id=0, has_side_effects=True, vmem_limit_bytes=60 * 2**20
        ),
    )(
        features, tile_values, tile_cols.reshape(1, n_slot), tile_rows.reshape(1, n_slot),
        tile_count, labels.reshape(1, rows_dev), w_self, w_neigh, w_out.T,
    )
    hidden, grad_self, grad_neigh, grad_out = pl.pallas_call(
        deliver,
        out_shape=(
            jax.ShapeDtypeStruct((rows_dev, HID), jnp.bfloat16),
            jax.ShapeDtypeStruct((F // 2, HID), jnp.float32),
            jax.ShapeDtypeStruct((F // 2, HID), jnp.float32),
            jax.ShapeDtypeStruct((C, HID // 2), jnp.float32),
        ),
        in_specs=[hbm] * 2,
        out_specs=(hbm,) * 4,
        scratch_shapes=[dma((6,))],
        compiler_params=pltpu.CompilerParams(vmem_limit_bytes=60 * 2**20),
    )(hidden, total)
    return hidden, grad_self, grad_neigh, grad_out.T


step_slots = 64


def aggregate(blocks_all, values, src_cols, dst_rows, live_count, rows_dev):
    slot_total = values.shape[0]
    dst_tiles = rows_dev // TB
    is_live = jnp.arange(slot_total) < live_count
    chosen = ((dst_rows[:, None] == jnp.arange(dst_tiles)[None, :]) & is_live[:, None]).astype(
        jnp.float32
    )
    turns = slot_total // step_slots
    tile_set = values.reshape(turns, step_slots, TB, TB)
    col_sets = src_cols.reshape(turns, step_slots)
    sel_sets = chosen.reshape(turns, step_slots, dst_tiles)

    def one_block(carry, pieces):
        tile_blk, col_blk, sel_blk = pieces
        gathered = blocks_all[col_blk]
        product = jnp.einsum("sij,sjf->sif", tile_blk, gathered, preferred_element_type=jnp.float32)
        total = carry[0] + jnp.einsum(
            "st,sif->tif", sel_blk, product, precision=lax.Precision.HIGHEST
        )
        row_sums = jnp.sum(tile_blk.astype(jnp.float32), axis=2)
        degree = carry[1] + jnp.einsum(
            "st,si->ti", sel_blk, row_sums, precision=lax.Precision.HIGHEST
        )
        return ((total, degree), None)

    start = (jnp.zeros((dst_tiles, TB, F), jnp.float32), jnp.zeros((dst_tiles, TB), jnp.float32))
    (total, degree), _ = lax.scan(one_block, start, (tile_set, col_sets, sel_sets))
    averaged = total / degree[:, :, None]
    return averaged.reshape(dst_tiles * TB, F).astype(jnp.bfloat16)


def local_wide(features, tile_values, tile_cols, tile_rows, tile_count, labels, w_self, w_neigh, w_out):
    rows_dev = labels.shape[0]
    n_row = lax.axis_size("row")
    n_rep = lax.axis_size("rep")
    rep_index = lax.axis_index("rep")
    own_rows = lax.dynamic_slice_in_dim(features, rep_index * rows_dev, rows_dev, 0)
    whole = lax.all_gather(features, "row", axis=0, tiled=True)
    blocks_all = whole.reshape(whole.shape[0] // TB, TB, F)
    neigh = aggregate(blocks_all, tile_values, tile_cols, tile_rows, tile_count[0], rows_dev)
    pre_act = jnp.dot(own_rows, w_self, preferred_element_type=jnp.float32) + jnp.dot(
        neigh, w_neigh, preferred_element_type=jnp.float32
    )
    hidden = jnp.maximum(pre_act, 0.0).astype(jnp.bfloat16)
    logits = jnp.dot(hidden, w_out, preferred_element_type=jnp.float32)
    row_max = jnp.max(logits, axis=1, keepdims=True)
    expo = jnp.exp(logits - row_max)
    probability = expo / jnp.sum(expo, axis=1, keepdims=True)
    one_hot = (labels[:, None] == jnp.arange(C)[None, :]).astype(jnp.float32)
    factor = 1.0 / math.sqrt(rows_dev * n_row * n_rep)
    d_logits = ((probability - one_hot) * factor).astype(jnp.bfloat16)
    part_out = jnp.dot(hidden.T, d_logits, preferred_element_type=jnp.float32)
    back = jnp.dot(d_logits, w_out.T, preferred_element_type=jnp.float32)
    d_pre = jnp.where(pre_act > 0.0, back, 0.0).astype(jnp.bfloat16)
    part_self = jnp.dot(own_rows.T, d_pre, preferred_element_type=jnp.float32)
    part_neigh = jnp.dot(neigh.T, d_pre, preferred_element_type=jnp.float32)
    summed = lax.psum((part_self, part_neigh, part_out), ("row", "rep"))
    feat_rows = F // n_rep
    hid_rows = HID // n_rep
    grad_self = lax.dynamic_slice_in_dim(summed[0], rep_index * feat_rows, feat_rows, 0)
    grad_neigh = lax.dynamic_slice_in_dim(summed[1], rep_index * feat_rows, feat_rows, 0)
    grad_out = lax.dynamic_slice_in_dim(summed[2], rep_index * hid_rows, hid_rows, 0)
    return (hidden, grad_self, grad_neigh, grad_out)


def solution(mesh):
    placed = (
        P(("parts", "row"), None),
        P(("parts", "row", "rep"), None),
        P(("parts", "row", "rep")),
        P(("parts", "row", "rep")),
        P(("parts", "row", "rep")),
        P(("parts", "row", "rep")),
        P(),
        P(),
        P(),
    )
    return jax.shard_map(
        local if mesh.shape["row"] <= 16 else local_wide,
        mesh=mesh,
        in_specs=placed,
        out_specs=(
            P(("parts", "row", "rep"), None),
            P(("parts", "rep"), None),
            P(("parts", "rep"), None),
            P(("parts", "rep"), None),
        ),
        check_vma=False,
    )
```

```python
import functools
import math

import jax
import jax.numpy as jnp
from jax import lax
from jax.experimental import pallas as pl
from jax.experimental.pallas import tpu as pltpu
from jax.sharding import PartitionSpec as P

F = 128
HID = 256
C = 172
TB = 64
LANES = 128
CHUNKS = 4
MESH = pl.DeviceIdType.MESH


def split_rows(n_row):
    first = 2 * F // n_row
    last = -(-C // (8 * n_row)) * 8
    return -(-(first + last + 8) // 16) * 16, (first + last) * n_row


def fused(
    n_row, feat_in, values, cols_in, rows_in, count, labels_in, w_self_in, w_neigh_in, w_out_in,
    hidden_out, total,
    feat, cols, rows, labels, w_self, w_neigh, w_out, in_sem, vbuf, spread, lhs, whole, order, part, got, held, codes, slots, everyone,
    v_sem, ga_send, ga_recv, gb_send, gb_recv, ra_send, ra_recv, rb_send, rb_recv, rc_send, rc_recv,
):
    me_part = lax.axis_index("parts")
    me_row = lax.axis_index("row")
    me_rep = lax.axis_index("rep")
    other = 1 - me_rep
    rows_dev = hidden_out.shape[0]
    dst_tiles = rows_dev // TB
    n_col = n_row * 2 * dst_tiles
    n_slot, tile_size = values.shape
    wide = tile_size // CHUNKS
    pairs = tile_size // LANES

    def peer(step):
        return lax.rem(me_row + step, n_row)

    def at(row, rep):
        return (me_part, row, rep)

    loads = [
        pltpu.make_async_copy(values.at[:, pl.ds(n * wide, wide)], vbuf.at[n], v_sem.at[n])
        for n in range(CHUNKS)
    ]
    inputs = [
        pltpu.make_async_copy(source, target, in_sem.at[n])
        for n, (source, target) in enumerate((
            (feat_in, feat), (cols_in, cols), (rows_in, rows), (labels_in, labels),
            (w_self_in, w_self), (w_neigh_in, w_neigh), (w_out_in, w_out),
        ))
    ]
    for copy in inputs[:3] + loads + inputs[3:]:
        copy.start()

    barrier = pltpu.get_barrier_semaphore()
    pl.semaphore_signal(barrier, inc=1, device_id=at(me_row, other), device_id_type=MESH)
    for step in range(1, n_row):
        pl.semaphore_signal(barrier, inc=1, device_id=at(peer(step), me_rep), device_id_type=MESH)
    pl.semaphore_wait(barrier, n_row)

    mine = pl.ds(pl.multiple_of(me_rep * rows_dev, rows_dev), rows_dev)
    across, beside = [], []
    for step in range(1, n_row):
        here = pl.ds(pl.multiple_of(me_row * 2 * rows_dev + me_rep * rows_dev, rows_dev), rows_dev)
        across.append(
            pltpu.make_async_remote_copy(
                feat.at[mine, :], whole.at[here, :], ga_send.at[step - 1], ga_recv.at[step - 1],
                device_id=at(peer(step), me_rep), device_id_type=MESH,
            )
        )
        source = lax.rem(me_row - step + n_row, n_row)
        came = pl.ds(pl.multiple_of(source * 2 * rows_dev + me_rep * rows_dev, rows_dev), rows_dev)
        beside.append(
            pltpu.make_async_remote_copy(
                whole.at[came, :], whole.at[came, :], gb_send.at[step - 1], gb_recv.at[step - 1],
                device_id=at(me_row, other), device_id_type=MESH,
            )
        )
    inputs[0].wait()
    for copy in across:
        copy.start()

    inputs[1].wait()
    inputs[2].wait()
    slot = lax.broadcasted_iota(jnp.int32, (1, n_slot), 1)
    place = jnp.where(slot < count[0], rows[...] * n_col + cols[...], -1)
    places = lax.broadcasted_iota(jnp.int32, (dst_tiles * n_col, n_slot), 0)
    pick = jnp.where(places == place, 1.0, 0.0).astype(jnp.bfloat16)
    per_chunk = pairs // CHUNKS
    for n in range(CHUNKS):
        loads[n].wait()
        block = jnp.dot(pick, vbuf[n], preferred_element_type=jnp.float32)
        for k in range(per_chunk):
            spread[pl.ds(n * per_chunk + k, dst_tiles * n_col, stride=pairs), :] = block[
                :, k * LANES : (k + 1) * LANES
            ]

    height = dst_tiles * pairs
    sums = jnp.zeros((height, LANES), jnp.float32)
    for c in range(n_col):
        piece = jnp.concatenate(
            [spread[pl.ds((t * n_col + c) * pairs, pairs), :] for t in range(dst_tiles)], axis=0
        )
        sums = sums + piece
        high = piece.astype(jnp.bfloat16)
        low = (piece - high.astype(jnp.float32)).astype(jnp.bfloat16)
        lhs[0:height, pl.ds(c * LANES, LANES)] = high
        lhs[height : 2 * height, pl.ds(c * LANES, LANES)] = low
    degree = (
        jnp.sum(sums[:, :TB], axis=1, keepdims=True),
        jnp.sum(sums[:, TB:], axis=1, keepdims=True),
    )

    for copy in inputs[3:]:
        copy.wait()
    own = feat[mine, :]
    pre_self = jnp.dot(own, w_self[...], preferred_element_type=jnp.float32)
    own_t = own.astype(jnp.float32).T.astype(jnp.bfloat16)
    class_at = lax.broadcasted_iota(jnp.int32, (C, rows_dev), 0)
    one_hot = jnp.where(class_at == labels[...], 1.0, 0.0).T

    zero = jnp.zeros((TB, F), jnp.bfloat16)

    def half(ref, start, row, rep):
        pieces = []
        for q in range(dst_tiles):
            x = ref[pl.ds(pl.multiple_of(start + q * TB, TB), TB), :]
            pieces.append(jnp.concatenate([x, zero], axis=1))
            pieces.append(jnp.concatenate([zero, x], axis=1))
        depth = dst_tiles * LANES
        left = lhs[:, pl.ds(pl.multiple_of((row * 2 + rep) * depth, depth), depth)]
        return jnp.dot(left, jnp.concatenate(pieces, axis=0), preferred_element_type=jnp.float32)

    acc = half(feat, 0, me_row, 0) + half(feat, rows_dev, me_row, 1)
    for step in range(1, n_row):
        across[step - 1].wait_recv()
        beside[step - 1].start()
        source = lax.rem(me_row - step + n_row, n_row)
        acc = acc + half(whole, source * 2 * rows_dev + me_rep * rows_dev, source, me_rep)
    for step in range(1, n_row):
        beside[step - 1].wait_recv()
        source = lax.rem(me_row - step + n_row, n_row)
        acc = acc + half(whole, source * 2 * rows_dev + other * rows_dev, source, other)
    agg = acc[:height] + acc[height:]
    for b in range(2):
        order[pl.ds(b, height, stride=2), :] = agg[:, b * F : (b + 1) * F] / degree[b]
    neigh_f = order[...].astype(jnp.bfloat16).astype(jnp.float32)
    neigh = neigh_f.astype(jnp.bfloat16)

    pre = pre_self + jnp.dot(neigh, w_neigh[...], preferred_element_type=jnp.float32)
    hidden = jnp.maximum(pre, 0.0).astype(jnp.bfloat16)
    hidden_out[...] = hidden
    logits = lax.dot_general(
        hidden, w_out[...], (((1,), (1,)), ((), ())), preferred_element_type=jnp.float32
    )
    expo = jnp.exp(logits - jnp.max(logits, axis=1, keepdims=True))
    probability = expo / jnp.sum(expo, axis=1, keepdims=True)
    factor = 1.0 / math.sqrt(rows_dev * n_row * 2)
    d_logits = ((probability - one_hot) * factor).astype(jnp.bfloat16)

    def to_partner(n, first, size):
        span = pl.ds(first, size)
        return pltpu.make_async_remote_copy(
            part.at[other, span, :], got.at[span, :], ra_send.at[n], ra_recv.at[n],
            device_id=at(me_row, other), device_id_type=MESH,
        )

    n_feat = F // 2
    top = 4 * n_feat
    all_rows = part.shape[1]
    sent = [to_partner(0, top, all_rows - top), to_partner(1, 0, 2 * n_feat), to_partner(2, 2 * n_feat, 2 * n_feat)]
    out_t = jnp.dot(
        d_logits.astype(jnp.float32).T.astype(jnp.bfloat16), hidden, preferred_element_type=jnp.float32
    )
    for h in range(2):
        part[h, top + C // 8 * 8 : all_rows, :] = jnp.zeros((all_rows - top - C // 8 * 8, LANES), jnp.float32)
        part[h, top : top + C, :] = out_t[:, h * LANES : (h + 1) * LANES]
    sent[0].start()
    back = jnp.dot(d_logits, w_out[...], preferred_element_type=jnp.float32)
    d_pre = jnp.where(pre > 0.0, back, 0.0).astype(jnp.bfloat16)
    for n, left in enumerate((own_t, neigh_f.T.astype(jnp.bfloat16))):
        grad = jnp.dot(left, d_pre, preferred_element_type=jnp.float32)
        for h in range(2):
            for b in range(2):
                part[h, pl.ds((2 * n + b) * n_feat, n_feat), :] = grad[
                    h * n_feat : (h + 1) * n_feat, b * LANES : (b + 1) * LANES
                ]
        sent[1 + n].start()

    spans = (pl.ds(top, all_rows - top), pl.ds(0, 2 * n_feat), pl.ds(2 * n_feat, 2 * n_feat))
    for n in range(3):
        sent[n].wait_recv()
        held[spans[n], :] = part[me_rep, spans[n], :] + got[spans[n], :]
    size = (2 * n_feat // n_row, 2 * n_feat // n_row, (all_rows - top) // n_row)
    base = (0, 2 * n_feat, top)

    def spans_of(row):
        return [pl.ds(pl.multiple_of(b + row * n, 8), n) for b, n in zip(base, size)]

    def encode(pieces):
        powers, whole_code = [], []
        for x in pieces:
            peak = jnp.maximum(jnp.max(jnp.abs(x), axis=0, keepdims=True), 1e-34)
            power = jnp.floor(jnp.log2(peak))
            powers.append(power)
            whole_code.append(jnp.floor(x * jnp.exp2(13.0 - power) + 0.5))
        line = lax.broadcasted_iota(jnp.int32, (8, LANES), 0)
        whole_code.append(jnp.where(line == 0, powers[0], jnp.where(line == 1, powers[1], powers[2])))
        spare = slots.shape[1] - sum(size) - 8
        if spare:
            whole_code.append(jnp.zeros((spare, LANES), jnp.float32))
        return jnp.concatenate(whole_code, axis=0).astype(jnp.int32).astype(jnp.int16)

    def decode(code):
        x = code.astype(jnp.int32).astype(jnp.float32)
        pieces, first, last = [], 0, sum(size)
        for n in range(3):
            pieces.append(x[first : first + size[n]] * jnp.exp2(x[last + n : last + n + 1] - 13.0))
            first += size[n]
        return pieces

    apart = []
    for step in range(1, n_row):
        codes[step - 1] = encode([held[span, :] for span in spans_of(peer(step))])
        apart.append(
            pltpu.make_async_remote_copy(
                codes.at[step - 1], slots.at[step - 1], rb_send.at[step - 1], rb_recv.at[step - 1],
                device_id=at(peer(step), me_rep), device_id_type=MESH,
            )
        )
        apart[-1].start()
    result = [held[span, :] for span in spans_of(me_row)]
    for step in range(1, n_row):
        apart[step - 1].wait_recv()
        result = [a + b for a, b in zip(result, decode(slots[step - 1]))]
    everyone[me_row] = encode(result)
    spreads = []
    for step in range(1, n_row):
        spreads.append(
            pltpu.make_async_remote_copy(
                everyone.at[me_row], everyone.at[me_row], rc_send.at[step - 1], rc_recv.at[step - 1],
                device_id=at(peer(step), me_rep), device_id_type=MESH,
            )
        )
        spreads[-1].start()
    for step in range(n_row):
        source = lax.rem(me_row - step + n_row, n_row)
        if step:
            pltpu.make_async_remote_copy(
                everyone.at[source], everyone.at[source], rc_send.at[step - 1], rc_recv.at[step - 1],
                device_id=at(peer(step), me_rep), device_id_type=MESH,
            ).wait_recv()
        for span, x in zip(spans_of(source), decode(everyone[source])):
            total[span, :] = x
    for copy in across + beside + sent + apart + spreads:
        copy.wait_send()


def deliver(hidden, total, hidden_out, gs_out, gn_out, go_out, near_hidden, near_total, in_sem, sem):
    top = 4 * gs_out.shape[0]
    cuts = [(hidden, near_hidden)] + [
        (total.at[a:b, :], near_total.at[a:b, :])
        for a, b in ((0, top // 2), (top // 2, top), (top, total.shape[0]))
    ]
    loads = [pltpu.make_async_copy(a, b, in_sem.at[n]) for n, (a, b) in enumerate(cuts)]
    for load in loads:
        load.start()
    n_feat = gs_out.shape[0]
    copies = [(near_hidden, hidden_out)]
    for n, out in enumerate((gs_out, gn_out)):
        for b in range(2):
            copies.append((
                near_total.at[pl.ds((2 * n + b) * n_feat, n_feat), :], out.at[:, pl.ds(b * LANES, LANES)]
            ))
    copies.append((near_total.at[pl.ds(4 * n_feat, C), :], go_out))
    moves = [pltpu.make_async_copy(a, b, sem.at[n]) for n, (a, b) in enumerate(copies)]
    for n, move in enumerate(moves):
        if n in (0, 1, 3, 5):
            loads[(n + 1) // 2].wait()
        move.start()
    for move in moves:
        move.wait()


def local(features, tile_values, tile_cols, tile_rows, tile_count, labels, w_self, w_neigh, w_out):
    rows_dev = labels.shape[0]
    n_row = lax.axis_size("row")
    n_slot, tile_size = tile_values.shape
    dst_tiles = rows_dev // TB
    n_col = n_row * 2 * dst_tiles
    pairs = tile_size // LANES
    each, all_rows = split_rows(n_row)
    vmem = pl.BlockSpec(memory_space=pltpu.VMEM)
    dma = pltpu.SemaphoreType.DMA
    peers = max(n_row - 1, 1)
    hbm = pl.BlockSpec(memory_space=pl.ANY)
    hidden, total = pl.pallas_call(
        functools.partial(fused, n_row),
        out_shape=(
            jax.ShapeDtypeStruct((rows_dev, HID), jnp.bfloat16),
            jax.ShapeDtypeStruct((all_rows, LANES), jnp.float32),
        ),
        in_specs=[hbm] * 4 + [pl.BlockSpec(memory_space=pltpu.SMEM)] + [hbm] * 4,
        out_specs=(vmem,) * 2,
        scratch_shapes=[
            pltpu.VMEM(features.shape, jnp.bfloat16),
            pltpu.VMEM((1, n_slot), jnp.int32),
            pltpu.VMEM((1, n_slot), jnp.int32),
            pltpu.VMEM((1, rows_dev), jnp.int32),
            pltpu.VMEM((F, HID), jnp.bfloat16),
            pltpu.VMEM((F, HID), jnp.bfloat16),
            pltpu.VMEM((C, HID), jnp.bfloat16),
            dma((7,)),
            pltpu.VMEM((CHUNKS, n_slot, tile_size // CHUNKS), jnp.bfloat16),
            pltpu.VMEM((dst_tiles * n_col * pairs, LANES), jnp.float32),
            pltpu.VMEM((2 * dst_tiles * pairs, n_col * LANES), jnp.bfloat16),
            pltpu.VMEM((n_row * 2 * rows_dev, F), jnp.bfloat16),
            pltpu.VMEM((rows_dev, F), jnp.float32),
            pltpu.VMEM((2, all_rows, LANES), jnp.float32),
            pltpu.VMEM((all_rows, LANES), jnp.float32),
            pltpu.VMEM((all_rows, LANES), jnp.float32),
            pltpu.VMEM((peers, each, LANES), jnp.int16),
            pltpu.VMEM((peers, each, LANES), jnp.int16),
            pltpu.VMEM((n_row, each, LANES), jnp.int16),
            dma((CHUNKS,)), dma((peers,)), dma((peers,)), dma((peers,)), dma((peers,)),
            dma((3,)), dma((3,)), dma((peers,)), dma((peers,)), dma((peers,)), dma((peers,)),
        ],
        compiler_params=pltpu.CompilerParams(
            collective_id=0, has_side_effects=True, vmem_limit_bytes=60 * 2**20
        ),
    )(
        features, tile_values, tile_cols.reshape(1, n_slot), tile_rows.reshape(1, n_slot),
        tile_count, labels.reshape(1, rows_dev), w_self, w_neigh, w_out.T,
    )
    hidden, grad_self, grad_neigh, grad_out = pl.pallas_call(
        deliver,
        out_shape=(
            jax.ShapeDtypeStruct((rows_dev, HID), jnp.bfloat16),
            jax.ShapeDtypeStruct((F // 2, HID), jnp.float32),
            jax.ShapeDtypeStruct((F // 2, HID), jnp.float32),
            jax.ShapeDtypeStruct((C, HID // 2), jnp.float32),
        ),
        in_specs=[hbm] * 2,
        out_specs=(hbm,) * 4,
        scratch_shapes=[
            pltpu.VMEM((rows_dev, HID), jnp.bfloat16),
            pltpu.VMEM((all_rows, LANES), jnp.float32),
            dma((4,)), dma((6,)),
        ],
        compiler_params=pltpu.CompilerParams(vmem_limit_bytes=60 * 2**20),
    )(hidden, total)
    return hidden, grad_self, grad_neigh, grad_out.T


step_slots = 64


def aggregate(blocks_all, values, src_cols, dst_rows, live_count, rows_dev):
    slot_total = values.shape[0]
    dst_tiles = rows_dev // TB
    is_live = jnp.arange(slot_total) < live_count
    chosen = ((dst_rows[:, None] == jnp.arange(dst_tiles)[None, :]) & is_live[:, None]).astype(
        jnp.float32
    )
    turns = slot_total // step_slots
    tile_set = values.reshape(turns, step_slots, TB, TB)
    col_sets = src_cols.reshape(turns, step_slots)
    sel_sets = chosen.reshape(turns, step_slots, dst_tiles)

    def one_block(carry, pieces):
        tile_blk, col_blk, sel_blk = pieces
        gathered = blocks_all[col_blk]
        product = jnp.einsum("sij,sjf->sif", tile_blk, gathered, preferred_element_type=jnp.float32)
        total = carry[0] + jnp.einsum(
            "st,sif->tif", sel_blk, product, precision=lax.Precision.HIGHEST
        )
        row_sums = jnp.sum(tile_blk.astype(jnp.float32), axis=2)
        degree = carry[1] + jnp.einsum(
            "st,si->ti", sel_blk, row_sums, precision=lax.Precision.HIGHEST
        )
        return ((total, degree), None)

    start = (jnp.zeros((dst_tiles, TB, F), jnp.float32), jnp.zeros((dst_tiles, TB), jnp.float32))
    (total, degree), _ = lax.scan(one_block, start, (tile_set, col_sets, sel_sets))
    averaged = total / degree[:, :, None]
    return averaged.reshape(dst_tiles * TB, F).astype(jnp.bfloat16)


def local_wide(features, tile_values, tile_cols, tile_rows, tile_count, labels, w_self, w_neigh, w_out):
    rows_dev = labels.shape[0]
    n_row = lax.axis_size("row")
    n_rep = lax.axis_size("rep")
    rep_index = lax.axis_index("rep")
    own_rows = lax.dynamic_slice_in_dim(features, rep_index * rows_dev, rows_dev, 0)
    whole = lax.all_gather(features, "row", axis=0, tiled=True)
    blocks_all = whole.reshape(whole.shape[0] // TB, TB, F)
    neigh = aggregate(blocks_all, tile_values, tile_cols, tile_rows, tile_count[0], rows_dev)
    pre_act = jnp.dot(own_rows, w_self, preferred_element_type=jnp.float32) + jnp.dot(
        neigh, w_neigh, preferred_element_type=jnp.float32
    )
    hidden = jnp.maximum(pre_act, 0.0).astype(jnp.bfloat16)
    logits = jnp.dot(hidden, w_out, preferred_element_type=jnp.float32)
    row_max = jnp.max(logits, axis=1, keepdims=True)
    expo = jnp.exp(logits - row_max)
    probability = expo / jnp.sum(expo, axis=1, keepdims=True)
    one_hot = (labels[:, None] == jnp.arange(C)[None, :]).astype(jnp.float32)
    factor = 1.0 / math.sqrt(rows_dev * n_row * n_rep)
    d_logits = ((probability - one_hot) * factor).astype(jnp.bfloat16)
    part_out = jnp.dot(hidden.T, d_logits, preferred_element_type=jnp.float32)
    back = jnp.dot(d_logits, w_out.T, preferred_element_type=jnp.float32)
    d_pre = jnp.where(pre_act > 0.0, back, 0.0).astype(jnp.bfloat16)
    part_self = jnp.dot(own_rows.T, d_pre, preferred_element_type=jnp.float32)
    part_neigh = jnp.dot(neigh.T, d_pre, preferred_element_type=jnp.float32)
    summed = lax.psum((part_self, part_neigh, part_out), ("row", "rep"))
    feat_rows = F // n_rep
    hid_rows = HID // n_rep
    grad_self = lax.dynamic_slice_in_dim(summed[0], rep_index * feat_rows, feat_rows, 0)
    grad_neigh = lax.dynamic_slice_in_dim(summed[1], rep_index * feat_rows, feat_rows, 0)
    grad_out = lax.dynamic_slice_in_dim(summed[2], rep_index * hid_rows, hid_rows, 0)
    return (hidden, grad_self, grad_neigh, grad_out)


def solution(mesh):
    placed = (
        P(("parts", "row"), None),
        P(("parts", "row", "rep"), None),
        P(("parts", "row", "rep")),
        P(("parts", "row", "rep")),
        P(("parts", "row", "rep")),
        P(("parts", "row", "rep")),
        P(),
        P(),
        P(),
    )
    return jax.shard_map(
        local if mesh.shape["row"] in (2, 4, 8) else local_wide,
        mesh=mesh,
        in_specs=placed,
        out_specs=(
            P(("parts", "row", "rep"), None),
            P(("parts", "rep"), None),
            P(("parts", "rep"), None),
            P(("parts", "rep"), None),
        ),
        check_vma=False,
    )
```

```python
import functools
import math

import jax
import jax.numpy as jnp
from jax import lax
from jax.experimental import pallas as pl
from jax.experimental.pallas import tpu as pltpu
from jax.sharding import PartitionSpec as P

F = 128
HID = 256
C = 172
TB = 64
LANES = 128
CHUNKS = 4
MESH = pl.DeviceIdType.MESH


def split_rows(n_row):
    first = 2 * F // n_row
    last = -(-C // (8 * n_row)) * 8
    return -(-(first + last + 8) // 16) * 16, (first + last) * n_row


def fused(
    n_row, feat_in, values, cols_in, rows_in, count, labels_in, w_self_in, w_neigh_in, w_out_in,
    hidden_out, total,
    feat, cols, rows, labels, w_self, w_neigh, w_out, in_sem, vbuf, spread, lhs, whole, order, part, got, held, codes, slots, everyone,
    v_sem, ga_send, ga_recv, gb_send, gb_recv, ra_send, ra_recv, rb_send, rb_recv, rc_send, rc_recv,
):
    me_part = lax.axis_index("parts")
    me_row = lax.axis_index("row")
    me_rep = lax.axis_index("rep")
    other = 1 - me_rep
    rows_dev = hidden_out.shape[0]
    dst_tiles = rows_dev // TB
    n_col = n_row * 2 * dst_tiles
    n_slot, tile_size = values.shape
    wide = tile_size // CHUNKS
    pairs = tile_size // LANES

    def peer(step):
        return lax.rem(me_row + step, n_row)

    def at(row, rep):
        return (me_part, row, rep)

    loads = [
        pltpu.make_async_copy(values.at[:, pl.ds(n * wide, wide)], vbuf.at[n], v_sem.at[n])
        for n in range(CHUNKS)
    ]
    inputs = [
        pltpu.make_async_copy(source, target, in_sem.at[n])
        for n, (source, target) in enumerate((
            (feat_in, feat), (cols_in, cols), (rows_in, rows), (labels_in, labels),
            (w_self_in, w_self), (w_neigh_in, w_neigh), (w_out_in, w_out),
        ))
    ]
    for copy in inputs[:3] + loads + inputs[3:]:
        copy.start()

    barrier = pltpu.get_barrier_semaphore()
    pl.semaphore_signal(barrier, inc=1, device_id=at(me_row, other), device_id_type=MESH)
    for step in range(1, n_row):
        pl.semaphore_signal(barrier, inc=1, device_id=at(peer(step), me_rep), device_id_type=MESH)
    pl.semaphore_wait(barrier, n_row)

    mine = pl.ds(pl.multiple_of(me_rep * rows_dev, rows_dev), rows_dev)
    across, beside = [], []
    for step in range(1, n_row):
        here = pl.ds(pl.multiple_of(me_row * 2 * rows_dev + me_rep * rows_dev, rows_dev), rows_dev)
        across.append(
            pltpu.make_async_remote_copy(
                feat.at[mine, :], whole.at[here, :], ga_send.at[step - 1], ga_recv.at[step - 1],
                device_id=at(peer(step), me_rep), device_id_type=MESH,
            )
        )
        source = lax.rem(me_row - step + n_row, n_row)
        came = pl.ds(pl.multiple_of(source * 2 * rows_dev + me_rep * rows_dev, rows_dev), rows_dev)
        beside.append(
            pltpu.make_async_remote_copy(
                whole.at[came, :], whole.at[came, :], gb_send.at[step - 1], gb_recv.at[step - 1],
                device_id=at(me_row, other), device_id_type=MESH,
            )
        )
    inputs[0].wait()
    for copy in across:
        copy.start()

    inputs[1].wait()
    inputs[2].wait()
    slot = lax.broadcasted_iota(jnp.int32, (1, n_slot), 1)
    place = jnp.where(slot < count[0], rows[...] * n_col + cols[...], -1)
    places = lax.broadcasted_iota(jnp.int32, (dst_tiles * n_col, n_slot), 0)
    pick = jnp.where(places == place, 1.0, 0.0).astype(jnp.bfloat16)
    per_chunk = pairs // CHUNKS
    for n in range(CHUNKS):
        loads[n].wait()
        block = jnp.dot(pick, vbuf[n], preferred_element_type=jnp.float32)
        for k in range(per_chunk):
            spread[pl.ds(n * per_chunk + k, dst_tiles * n_col, stride=pairs), :] = block[
                :, k * LANES : (k + 1) * LANES
            ]

    height = dst_tiles * pairs
    sums = jnp.zeros((height, LANES), jnp.float32)
    for c in range(n_col):
        piece = jnp.concatenate(
            [spread[pl.ds((t * n_col + c) * pairs, pairs), :] for t in range(dst_tiles)], axis=0
        )
        sums = sums + piece
        high = piece.astype(jnp.bfloat16)
        low = (piece - high.astype(jnp.float32)).astype(jnp.bfloat16)
        lhs[0:height, pl.ds(c * LANES, LANES)] = high
        lhs[height : 2 * height, pl.ds(c * LANES, LANES)] = low
    degree = (
        jnp.sum(sums[:, :TB], axis=1, keepdims=True),
        jnp.sum(sums[:, TB:], axis=1, keepdims=True),
    )

    for copy in inputs[3:]:
        copy.wait()
    own = feat[mine, :]
    pre_self = jnp.dot(own, w_self[...], preferred_element_type=jnp.float32)
    own_t = own.astype(jnp.float32).T.astype(jnp.bfloat16)
    class_at = lax.broadcasted_iota(jnp.int32, (C, rows_dev), 0)
    one_hot = jnp.where(class_at == labels[...], 1.0, 0.0).T

    zero = jnp.zeros((TB, F), jnp.bfloat16)

    def half(ref, start, row, rep):
        pieces = []
        for q in range(dst_tiles):
            x = ref[pl.ds(pl.multiple_of(start + q * TB, TB), TB), :]
            pieces.append(jnp.concatenate([x, zero], axis=1))
            pieces.append(jnp.concatenate([zero, x], axis=1))
        depth = dst_tiles * LANES
        left = lhs[:, pl.ds(pl.multiple_of((row * 2 + rep) * depth, depth), depth)]
        return jnp.dot(left, jnp.concatenate(pieces, axis=0), preferred_element_type=jnp.float32)

    acc = half(feat, 0, me_row, 0) + half(feat, rows_dev, me_row, 1)
    for step in range(1, n_row):
        across[step - 1].wait_recv()
        beside[step - 1].start()
        source = lax.rem(me_row - step + n_row, n_row)
        acc = acc + half(whole, source * 2 * rows_dev + me_rep * rows_dev, source, me_rep)
    for step in range(1, n_row):
        beside[step - 1].wait_recv()
        source = lax.rem(me_row - step + n_row, n_row)
        acc = acc + half(whole, source * 2 * rows_dev + other * rows_dev, source, other)
    agg = acc[:height] + acc[height:]
    for b in range(2):
        order[pl.ds(b, height, stride=2), :] = agg[:, b * F : (b + 1) * F] / degree[b]
    neigh_f = order[...].astype(jnp.bfloat16).astype(jnp.float32)
    neigh = neigh_f.astype(jnp.bfloat16)

    pre = pre_self + jnp.dot(neigh, w_neigh[...], preferred_element_type=jnp.float32)
    hidden = jnp.maximum(pre, 0.0).astype(jnp.bfloat16)
    hidden_out[...] = hidden
    logits = lax.dot_general(
        hidden, w_out[...], (((1,), (1,)), ((), ())), preferred_element_type=jnp.float32
    )
    expo = jnp.exp(logits - jnp.max(logits, axis=1, keepdims=True))
    probability = expo / jnp.sum(expo, axis=1, keepdims=True)
    factor = 1.0 / math.sqrt(rows_dev * n_row * 2)
    d_logits = ((probability - one_hot) * factor).astype(jnp.bfloat16)

    def to_partner(n, first, size):
        span = pl.ds(first, size)
        return pltpu.make_async_remote_copy(
            part.at[other, span, :], got.at[span, :], ra_send.at[n], ra_recv.at[n],
            device_id=at(me_row, other), device_id_type=MESH,
        )

    n_feat = F // 2
    top = 4 * n_feat
    all_rows = part.shape[1]
    sent = [to_partner(0, top, all_rows - top), to_partner(1, 0, 2 * n_feat), to_partner(2, 2 * n_feat, 2 * n_feat)]
    out_t = jnp.dot(
        d_logits.astype(jnp.float32).T.astype(jnp.bfloat16), hidden, preferred_element_type=jnp.float32
    )
    for h in range(2):
        part[h, top + C // 8 * 8 : all_rows, :] = jnp.zeros((all_rows - top - C // 8 * 8, LANES), jnp.float32)
        part[h, top : top + C, :] = out_t[:, h * LANES : (h + 1) * LANES]
    sent[0].start()
    back = jnp.dot(d_logits, w_out[...], preferred_element_type=jnp.float32)
    d_pre = jnp.where(pre > 0.0, back, 0.0).astype(jnp.bfloat16)
    for n, left in enumerate((own_t, neigh_f.T.astype(jnp.bfloat16))):
        grad = jnp.dot(left, d_pre, preferred_element_type=jnp.float32)
        for h in range(2):
            for b in range(2):
                part[h, pl.ds((2 * n + b) * n_feat, n_feat), :] = grad[
                    h * n_feat : (h + 1) * n_feat, b * LANES : (b + 1) * LANES
                ]
        sent[1 + n].start()

    spans = (pl.ds(top, all_rows - top), pl.ds(0, 2 * n_feat), pl.ds(2 * n_feat, 2 * n_feat))
    for n in range(3):
        sent[n].wait_recv()
        held[spans[n], :] = part[me_rep, spans[n], :] + got[spans[n], :]
    size = (2 * n_feat // n_row, 2 * n_feat // n_row, (all_rows - top) // n_row)
    base = (0, 2 * n_feat, top)

    def spans_of(row):
        return [pl.ds(pl.multiple_of(b + row * n, 8), n) for b, n in zip(base, size)]

    def encode(pieces):
        powers, whole_code = [], []
        for x in pieces:
            peak = jnp.maximum(jnp.max(jnp.abs(x), axis=0, keepdims=True), 1e-34)
            power = jnp.floor(jnp.log2(peak))
            powers.append(power)
            whole_code.append(jnp.floor(x * jnp.exp2(13.0 - power) + 0.5))
        line = lax.broadcasted_iota(jnp.int32, (8, LANES), 0)
        whole_code.append(jnp.where(line == 0, powers[0], jnp.where(line == 1, powers[1], powers[2])))
        spare = slots.shape[1] - sum(size) - 8
        if spare:
            whole_code.append(jnp.zeros((spare, LANES), jnp.float32))
        return jnp.concatenate(whole_code, axis=0).astype(jnp.int32).astype(jnp.int16)

    def decode(code):
        x = code.astype(jnp.int32).astype(jnp.float32)
        pieces, first, last = [], 0, sum(size)
        for n in range(3):
            pieces.append(x[first : first + size[n]] * jnp.exp2(x[last + n : last + n + 1] - 13.0))
            first += size[n]
        return pieces

    apart = []
    for step in range(1, n_row):
        codes[step - 1] = encode([held[span, :] for span in spans_of(peer(step))])
        apart.append(
            pltpu.make_async_remote_copy(
                codes.at[step - 1], slots.at[step - 1], rb_send.at[step - 1], rb_recv.at[step - 1],
                device_id=at(peer(step), me_rep), device_id_type=MESH,
            )
        )
        apart[-1].start()
    result = [held[span, :] for span in spans_of(me_row)]
    for step in range(1, n_row):
        apart[step - 1].wait_recv()
        result = [a + b for a, b in zip(result, decode(slots[step - 1]))]
    everyone[me_row] = encode(result)
    spreads = []
    for step in range(1, n_row):
        spreads.append(
            pltpu.make_async_remote_copy(
                everyone.at[me_row], everyone.at[me_row], rc_send.at[step - 1], rc_recv.at[step - 1],
                device_id=at(peer(step), me_rep), device_id_type=MESH,
            )
        )
        spreads[-1].start()
    for step in range(n_row):
        source = lax.rem(me_row - step + n_row, n_row)
        if step:
            pltpu.make_async_remote_copy(
                everyone.at[source], everyone.at[source], rc_send.at[step - 1], rc_recv.at[step - 1],
                device_id=at(peer(step), me_rep), device_id_type=MESH,
            ).wait_recv()
        for span, x in zip(spans_of(source), decode(everyone[source])):
            total[span, :] = x
    for copy in across + beside + sent + apart + spreads:
        copy.wait_send()


def deliver(hidden, total, hidden_out, gs_out, gn_out, go_out, sem):
    n_feat = gs_out.shape[0]
    copies = [(hidden, hidden_out)]
    for n, out in enumerate((gs_out, gn_out)):
        for b in range(2):
            copies.append((
                total.at[pl.ds((2 * n + b) * n_feat, n_feat), :], out.at[:, pl.ds(b * LANES, LANES)]
            ))
    copies.append((total.at[pl.ds(4 * n_feat, C), :], go_out))
    moves = [pltpu.make_async_copy(a, b, sem.at[n]) for n, (a, b) in enumerate(copies)]
    for move in moves:
        move.start()
    for move in moves:
        move.wait()


def local(features, tile_values, tile_cols, tile_rows, tile_count, labels, w_self, w_neigh, w_out):
    rows_dev = labels.shape[0]
    n_row = lax.axis_size("row")
    n_slot, tile_size = tile_values.shape
    dst_tiles = rows_dev // TB
    n_col = n_row * 2 * dst_tiles
    pairs = tile_size // LANES
    each, all_rows = split_rows(n_row)
    vmem = pl.BlockSpec(memory_space=pltpu.VMEM)
    dma = pltpu.SemaphoreType.DMA
    peers = max(n_row - 1, 1)
    hbm = pl.BlockSpec(memory_space=pl.ANY)
    hidden, total = pl.pallas_call(
        functools.partial(fused, n_row),
        out_shape=(
            pltpu.VMEM((rows_dev, HID), jnp.bfloat16),
            pltpu.VMEM((all_rows, LANES), jnp.float32),
        ),
        in_specs=[hbm] * 4 + [pl.BlockSpec(memory_space=pltpu.SMEM)] + [hbm] * 4,
        out_specs=(vmem,) * 2,
        scratch_shapes=[
            pltpu.VMEM(features.shape, jnp.bfloat16),
            pltpu.VMEM((1, n_slot), jnp.int32),
            pltpu.VMEM((1, n_slot), jnp.int32),
            pltpu.VMEM((1, rows_dev), jnp.int32),
            pltpu.VMEM((F, HID), jnp.bfloat16),
            pltpu.VMEM((F, HID), jnp.bfloat16),
            pltpu.VMEM((C, HID), jnp.bfloat16),
            dma((7,)),
            pltpu.VMEM((CHUNKS, n_slot, tile_size // CHUNKS), jnp.bfloat16),
            pltpu.VMEM((dst_tiles * n_col * pairs, LANES), jnp.float32),
            pltpu.VMEM((2 * dst_tiles * pairs, n_col * LANES), jnp.bfloat16),
            pltpu.VMEM((n_row * 2 * rows_dev, F), jnp.bfloat16),
            pltpu.VMEM((rows_dev, F), jnp.float32),
            pltpu.VMEM((2, all_rows, LANES), jnp.float32),
            pltpu.VMEM((all_rows, LANES), jnp.float32),
            pltpu.VMEM((all_rows, LANES), jnp.float32),
            pltpu.VMEM((peers, each, LANES), jnp.int16),
            pltpu.VMEM((peers, each, LANES), jnp.int16),
            pltpu.VMEM((n_row, each, LANES), jnp.int16),
            dma((CHUNKS,)), dma((peers,)), dma((peers,)), dma((peers,)), dma((peers,)),
            dma((3,)), dma((3,)), dma((peers,)), dma((peers,)), dma((peers,)), dma((peers,)),
        ],
        compiler_params=pltpu.CompilerParams(
            collective_id=0, has_side_effects=True, vmem_limit_bytes=60 * 2**20
        ),
    )(
        features, tile_values, tile_cols.reshape(1, n_slot), tile_rows.reshape(1, n_slot),
        tile_count, labels.reshape(1, rows_dev), w_self, w_neigh, w_out.T,
    )
    hidden, grad_self, grad_neigh, grad_out = pl.pallas_call(
        deliver,
        out_shape=(
            jax.ShapeDtypeStruct((rows_dev, HID), jnp.bfloat16),
            jax.ShapeDtypeStruct((F // 2, HID), jnp.float32),
            jax.ShapeDtypeStruct((F // 2, HID), jnp.float32),
            jax.ShapeDtypeStruct((C, HID // 2), jnp.float32),
        ),
        in_specs=[vmem] * 2,
        out_specs=(hbm,) * 4,
        scratch_shapes=[dma((6,))],
        compiler_params=pltpu.CompilerParams(vmem_limit_bytes=2**20),
    )(hidden, total)
    return hidden, grad_self, grad_neigh, grad_out.T


step_slots = 64


def aggregate(blocks_all, values, src_cols, dst_rows, live_count, rows_dev):
    slot_total = values.shape[0]
    dst_tiles = rows_dev // TB
    is_live = jnp.arange(slot_total) < live_count
    chosen = ((dst_rows[:, None] == jnp.arange(dst_tiles)[None, :]) & is_live[:, None]).astype(
        jnp.float32
    )
    turns = slot_total // step_slots
    tile_set = values.reshape(turns, step_slots, TB, TB)
    col_sets = src_cols.reshape(turns, step_slots)
    sel_sets = chosen.reshape(turns, step_slots, dst_tiles)

    def one_block(carry, pieces):
        tile_blk, col_blk, sel_blk = pieces
        gathered = blocks_all[col_blk]
        product = jnp.einsum("sij,sjf->sif", tile_blk, gathered, preferred_element_type=jnp.float32)
        total = carry[0] + jnp.einsum(
            "st,sif->tif", sel_blk, product, precision=lax.Precision.HIGHEST
        )
        row_sums = jnp.sum(tile_blk.astype(jnp.float32), axis=2)
        degree = carry[1] + jnp.einsum(
            "st,si->ti", sel_blk, row_sums, precision=lax.Precision.HIGHEST
        )
        return ((total, degree), None)

    start = (jnp.zeros((dst_tiles, TB, F), jnp.float32), jnp.zeros((dst_tiles, TB), jnp.float32))
    (total, degree), _ = lax.scan(one_block, start, (tile_set, col_sets, sel_sets))
    averaged = total / degree[:, :, None]
    return averaged.reshape(dst_tiles * TB, F).astype(jnp.bfloat16)


def local_wide(features, tile_values, tile_cols, tile_rows, tile_count, labels, w_self, w_neigh, w_out):
    rows_dev = labels.shape[0]
    n_row = lax.axis_size("row")
    n_rep = lax.axis_size("rep")
    rep_index = lax.axis_index("rep")
    own_rows = lax.dynamic_slice_in_dim(features, rep_index * rows_dev, rows_dev, 0)
    whole = lax.all_gather(features, "row", axis=0, tiled=True)
    blocks_all = whole.reshape(whole.shape[0] // TB, TB, F)
    neigh = aggregate(blocks_all, tile_values, tile_cols, tile_rows, tile_count[0], rows_dev)
    pre_act = jnp.dot(own_rows, w_self, preferred_element_type=jnp.float32) + jnp.dot(
        neigh, w_neigh, preferred_element_type=jnp.float32
    )
    hidden = jnp.maximum(pre_act, 0.0).astype(jnp.bfloat16)
    logits = jnp.dot(hidden, w_out, preferred_element_type=jnp.float32)
    row_max = jnp.max(logits, axis=1, keepdims=True)
    expo = jnp.exp(logits - row_max)
    probability = expo / jnp.sum(expo, axis=1, keepdims=True)
    one_hot = (labels[:, None] == jnp.arange(C)[None, :]).astype(jnp.float32)
    factor = 1.0 / math.sqrt(rows_dev * n_row * n_rep)
    d_logits = ((probability - one_hot) * factor).astype(jnp.bfloat16)
    part_out = jnp.dot(hidden.T, d_logits, preferred_element_type=jnp.float32)
    back = jnp.dot(d_logits, w_out.T, preferred_element_type=jnp.float32)
    d_pre = jnp.where(pre_act > 0.0, back, 0.0).astype(jnp.bfloat16)
    part_self = jnp.dot(own_rows.T, d_pre, preferred_element_type=jnp.float32)
    part_neigh = jnp.dot(neigh.T, d_pre, preferred_element_type=jnp.float32)
    summed = lax.psum((part_self, part_neigh, part_out), ("row", "rep"))
    feat_rows = F // n_rep
    hid_rows = HID // n_rep
    grad_self = lax.dynamic_slice_in_dim(summed[0], rep_index * feat_rows, feat_rows, 0)
    grad_neigh = lax.dynamic_slice_in_dim(summed[1], rep_index * feat_rows, feat_rows, 0)
    grad_out = lax.dynamic_slice_in_dim(summed[2], rep_index * hid_rows, hid_rows, 0)
    return (hidden, grad_self, grad_neigh, grad_out)


def solution(mesh):
    placed = (
        P(("parts", "row"), None),
        P(("parts", "row", "rep"), None),
        P(("parts", "row", "rep")),
        P(("parts", "row", "rep")),
        P(("parts", "row", "rep")),
        P(("parts", "row", "rep")),
        P(),
        P(),
        P(),
    )
    return jax.shard_map(
        local if mesh.shape["row"] in (2, 4, 8) else local_wide,
        mesh=mesh,
        in_specs=placed,
        out_specs=(
            P(("parts", "row", "rep"), None),
            P(("parts", "rep"), None),
            P(("parts", "rep"), None),
            P(("parts", "rep"), None),
        ),
        check_vma=False,
    )
```

```python
import functools
import math

import jax
import jax.numpy as jnp
from jax import lax
from jax.experimental import pallas as pl
from jax.experimental.pallas import tpu as pltpu
from jax.sharding import PartitionSpec as P

F = 128
HID = 256
C = 172
TB = 64
LANES = 128
CHUNKS = 4
MESH = pl.DeviceIdType.MESH


def split_rows(n_row):
    first = 2 * F // n_row
    last = -(-C // (8 * n_row)) * 8
    return -(-(first + last + 8) // 16) * 16, (first + last) * n_row


def fused(
    n_row, feat_in, values, cols_in, rows_in, count, labels_in, w_self_in, w_neigh_in, w_out_in,
    hidden_out, total,
    feat, cols, rows, labels, w_self, w_neigh, w_out, in_sem, vbuf, spread, lhs, whole, order, part, got, held, codes, slots, everyone,
    v_sem, ga_send, ga_recv, gb_send, gb_recv, ra_send, ra_recv, rb_send, rb_recv, rc_send, rc_recv,
):
    me_part = lax.axis_index("parts")
    me_row = lax.axis_index("row")
    me_rep = lax.axis_index("rep")
    other = 1 - me_rep
    rows_dev = hidden_out.shape[0]
    dst_tiles = rows_dev // TB
    n_col = n_row * 2 * dst_tiles
    n_slot, tile_size = values.shape
    wide = tile_size // CHUNKS
    pairs = tile_size // LANES

    def peer(step):
        return lax.rem(me_row + step, n_row)

    def at(row, rep):
        return (me_part, row, rep)

    loads = [
        pltpu.make_async_copy(values.at[:, pl.ds(n * wide, wide)], vbuf.at[n], v_sem.at[n])
        for n in range(CHUNKS)
    ]
    inputs = [
        pltpu.make_async_copy(source, target, in_sem.at[n])
        for n, (source, target) in enumerate((
            (feat_in, feat), (cols_in, cols), (rows_in, rows), (labels_in, labels),
            (w_self_in, w_self), (w_neigh_in, w_neigh), (w_out_in, w_out),
        ))
    ]
    for copy in inputs[:3] + loads + inputs[3:]:
        copy.start()

    barrier = pltpu.get_barrier_semaphore()
    pl.semaphore_signal(barrier, inc=1, device_id=at(me_row, other), device_id_type=MESH)
    for step in range(1, n_row):
        pl.semaphore_signal(barrier, inc=1, device_id=at(peer(step), me_rep), device_id_type=MESH)
    pl.semaphore_wait(barrier, n_row)

    mine = pl.ds(pl.multiple_of(me_rep * rows_dev, rows_dev), rows_dev)
    across, beside = [], []
    for step in range(1, n_row):
        here = pl.ds(pl.multiple_of(me_row * 2 * rows_dev + me_rep * rows_dev, rows_dev), rows_dev)
        across.append(
            pltpu.make_async_remote_copy(
                feat.at[mine, :], whole.at[here, :], ga_send.at[step - 1], ga_recv.at[step - 1],
                device_id=at(peer(step), me_rep), device_id_type=MESH,
            )
        )
        source = lax.rem(me_row - step + n_row, n_row)
        came = pl.ds(pl.multiple_of(source * 2 * rows_dev + me_rep * rows_dev, rows_dev), rows_dev)
        beside.append(
            pltpu.make_async_remote_copy(
                whole.at[came, :], whole.at[came, :], gb_send.at[step - 1], gb_recv.at[step - 1],
                device_id=at(me_row, other), device_id_type=MESH,
            )
        )
    inputs[0].wait()
    for copy in across:
        copy.start()

    inputs[1].wait()
    inputs[2].wait()
    slot = lax.broadcasted_iota(jnp.int32, (1, n_slot), 1)
    place = jnp.where(slot < count[0], rows[...] * n_col + cols[...], -1)
    places = lax.broadcasted_iota(jnp.int32, (dst_tiles * n_col, n_slot), 0)
    pick = jnp.where(places == place, 1.0, 0.0).astype(jnp.bfloat16)
    per_chunk = pairs // CHUNKS
    for n in range(CHUNKS):
        loads[n].wait()
        block = jnp.dot(pick, vbuf[n], preferred_element_type=jnp.float32)
        for k in range(per_chunk):
            spread[pl.ds(n * per_chunk + k, dst_tiles * n_col, stride=pairs), :] = block[
                :, k * LANES : (k + 1) * LANES
            ]

    height = dst_tiles * pairs
    sums = jnp.zeros((height, LANES), jnp.float32)
    for c in range(n_col):
        piece = jnp.concatenate(
            [spread[pl.ds((t * n_col + c) * pairs, pairs), :] for t in range(dst_tiles)], axis=0
        )
        sums = sums + piece
        high = piece.astype(jnp.bfloat16)
        low = (piece - high.astype(jnp.float32)).astype(jnp.bfloat16)
        lhs[0:height, pl.ds(c * LANES, LANES)] = high
        lhs[height : 2 * height, pl.ds(c * LANES, LANES)] = low
    degree = (
        jnp.sum(sums[:, :TB], axis=1, keepdims=True),
        jnp.sum(sums[:, TB:], axis=1, keepdims=True),
    )

    for copy in inputs[3:]:
        copy.wait()
    own = feat[mine, :]
    pre_self = jnp.dot(own, w_self[...], preferred_element_type=jnp.float32)
    own_t = own.astype(jnp.float32).T.astype(jnp.bfloat16)
    class_at = lax.broadcasted_iota(jnp.int32, (C, rows_dev), 0)
    one_hot = jnp.where(class_at == labels[...], 1.0, 0.0).T

    zero = jnp.zeros((TB, F), jnp.bfloat16)

    def half(ref, start, row, rep):
        pieces = []
        for q in range(dst_tiles):
            x = ref[pl.ds(pl.multiple_of(start + q * TB, TB), TB), :]
            pieces.append(jnp.concatenate([x, zero], axis=1))
            pieces.append(jnp.concatenate([zero, x], axis=1))
        depth = dst_tiles * LANES
        left = lhs[:, pl.ds(pl.multiple_of((row * 2 + rep) * depth, depth), depth)]
        return jnp.dot(left, jnp.concatenate(pieces, axis=0), preferred_element_type=jnp.float32)

    acc = half(feat, 0, me_row, 0) + half(feat, rows_dev, me_row, 1)
    for step in range(1, n_row):
        across[step - 1].wait_recv()
        beside[step - 1].start()
        source = lax.rem(me_row - step + n_row, n_row)
        acc = acc + half(whole, source * 2 * rows_dev + me_rep * rows_dev, source, me_rep)
    for step in range(1, n_row):
        beside[step - 1].wait_recv()
        source = lax.rem(me_row - step + n_row, n_row)
        acc = acc + half(whole, source * 2 * rows_dev + other * rows_dev, source, other)
    agg = acc[:height] + acc[height:]
    for b in range(2):
        order[pl.ds(b, height, stride=2), :] = agg[:, b * F : (b + 1) * F] / degree[b]
    neigh_f = order[...].astype(jnp.bfloat16).astype(jnp.float32)
    neigh = neigh_f.astype(jnp.bfloat16)

    pre = pre_self + jnp.dot(neigh, w_neigh[...], preferred_element_type=jnp.float32)
    hidden = jnp.maximum(pre, 0.0).astype(jnp.bfloat16)
    hidden_out[...] = hidden
    logits = lax.dot_general(
        hidden, w_out[...], (((1,), (1,)), ((), ())), preferred_element_type=jnp.float32
    )
    expo = jnp.exp(logits - jnp.max(logits, axis=1, keepdims=True))
    probability = expo / jnp.sum(expo, axis=1, keepdims=True)
    factor = 1.0 / math.sqrt(rows_dev * n_row * 2)
    d_logits = ((probability - one_hot) * factor).astype(jnp.bfloat16)

    def to_partner(n, first, size):
        span = pl.ds(first, size)
        return pltpu.make_async_remote_copy(
            part.at[other, span, :], got.at[span, :], ra_send.at[n], ra_recv.at[n],
            device_id=at(me_row, other), device_id_type=MESH,
        )

    n_feat = F // 2
    top = 4 * n_feat
    all_rows = part.shape[1]
    sent = [to_partner(0, top, all_rows - top), to_partner(1, 0, 2 * n_feat), to_partner(2, 2 * n_feat, 2 * n_feat)]
    back = jnp.dot(d_logits, w_out[...], preferred_element_type=jnp.float32)
    d_pre = jnp.where(pre > 0.0, back, 0.0).astype(jnp.bfloat16)
    out_t = jnp.dot(
        d_logits.astype(jnp.float32).T.astype(jnp.bfloat16), hidden, preferred_element_type=jnp.float32
    )
    for h in range(2):
        part[h, top + C // 8 * 8 : all_rows, :] = jnp.zeros((all_rows - top - C // 8 * 8, LANES), jnp.float32)
        part[h, top : top + C, :] = out_t[:, h * LANES : (h + 1) * LANES]
    sent[0].start()
    for n, left in enumerate((own_t, neigh_f.T.astype(jnp.bfloat16))):
        grad = jnp.dot(left, d_pre, preferred_element_type=jnp.float32)
        for h in range(2):
            for b in range(2):
                part[h, pl.ds((2 * n + b) * n_feat, n_feat), :] = grad[
                    h * n_feat : (h + 1) * n_feat, b * LANES : (b + 1) * LANES
                ]
        sent[1 + n].start()

    spans = (pl.ds(top, all_rows - top), pl.ds(0, 2 * n_feat), pl.ds(2 * n_feat, 2 * n_feat))
    for n in range(3):
        sent[n].wait_recv()
        held[spans[n], :] = part[me_rep, spans[n], :] + got[spans[n], :]
    size = (2 * n_feat // n_row, 2 * n_feat // n_row, (all_rows - top) // n_row)
    base = (0, 2 * n_feat, top)

    def encode(pieces):
        powers, whole_code = [], []
        for x in pieces:
            peak = jnp.maximum(jnp.max(jnp.abs(x), axis=1, keepdims=True), 1e-34)
            power = jnp.floor(jnp.log2(peak))
            powers.append(power)
            whole_code.append(jnp.floor(x * jnp.exp2(13.0 - power) + 0.5))
        count_of = pieces[0].shape[0]
        line = lax.broadcasted_iota(jnp.int32, (count_of, 8, LANES), 1)
        whole_code.append(jnp.where(line == 0, powers[0], jnp.where(line == 1, powers[1], powers[2])))
        spare = slots.shape[1] - sum(size) - 8
        if spare:
            whole_code.append(jnp.zeros((count_of, spare, LANES), jnp.float32))
        return jnp.concatenate(whole_code, axis=1).astype(jnp.int32).astype(jnp.int16)

    def decode(code):
        x = code.astype(jnp.int32).astype(jnp.float32)
        pieces, first, last = [], 0, sum(size)
        for n in range(3):
            scale = jnp.exp2(x[:, last + n : last + n + 1] - 13.0)
            pieces.append(x[:, first : first + size[n]] * scale)
            first += size[n]
        return pieces

    codes[...] = encode([
        held[b : b + n_row * n, :].reshape(n_row, n, LANES) for b, n in zip(base, size)
    ])
    apart = []
    for step in range(1, n_row):
        apart.append(
            pltpu.make_async_remote_copy(
                codes.at[peer(step)], slots.at[step - 1], rb_send.at[step - 1], rb_recv.at[step - 1],
                device_id=at(peer(step), me_rep), device_id_type=MESH,
            )
        )
        apart[-1].start()
    result = [
        held[pl.ds(pl.multiple_of(b + me_row * n, 8), n), :] for b, n in zip(base, size)
    ]
    for copy in apart:
        copy.wait_recv()
    result = [a + jnp.sum(b, axis=0) for a, b in zip(result, decode(slots[...]))]
    everyone[me_row] = encode([x[None] for x in result])[0]
    spreads = []
    for step in range(1, n_row):
        spreads.append(
            pltpu.make_async_remote_copy(
                everyone.at[me_row], everyone.at[me_row], rc_send.at[step - 1], rc_recv.at[step - 1],
                device_id=at(peer(step), me_rep), device_id_type=MESH,
            )
        )
        spreads[-1].start()
    for step in range(1, n_row):
        source = lax.rem(me_row - step + n_row, n_row)
        pltpu.make_async_remote_copy(
            everyone.at[source], everyone.at[source], rc_send.at[step - 1], rc_recv.at[step - 1],
            device_id=at(peer(step), me_rep), device_id_type=MESH,
        ).wait_recv()
    for b, n, x in zip(base, size, decode(everyone[...])):
        total[b : b + n_row * n, :] = x.reshape(n_row * n, LANES)
    for copy in across + beside + sent + apart + spreads:
        copy.wait_send()


def deliver(hidden, total, hidden_out, gs_out, gn_out, go_out, sem):
    n_feat = gs_out.shape[0]
    copies = [(hidden, hidden_out)]
    for n, out in enumerate((gs_out, gn_out)):
        for b in range(2):
            copies.append((
                total.at[pl.ds((2 * n + b) * n_feat, n_feat), :], out.at[:, pl.ds(b * LANES, LANES)]
            ))
    copies.append((total.at[pl.ds(4 * n_feat, C), :], go_out))
    moves = [pltpu.make_async_copy(a, b, sem.at[n]) for n, (a, b) in enumerate(copies)]
    for move in moves:
        move.start()
    for move in moves:
        move.wait()


def local(features, tile_values, tile_cols, tile_rows, tile_count, labels, w_self, w_neigh, w_out):
    rows_dev = labels.shape[0]
    n_row = lax.axis_size("row")
    n_slot, tile_size = tile_values.shape
    dst_tiles = rows_dev // TB
    n_col = n_row * 2 * dst_tiles
    pairs = tile_size // LANES
    each, all_rows = split_rows(n_row)
    vmem = pl.BlockSpec(memory_space=pltpu.VMEM)
    dma = pltpu.SemaphoreType.DMA
    peers = max(n_row - 1, 1)
    hbm = pl.BlockSpec(memory_space=pl.ANY)
    hidden, total = pl.pallas_call(
        functools.partial(fused, n_row),
        out_shape=(
            pltpu.VMEM((rows_dev, HID), jnp.bfloat16),
            pltpu.VMEM((all_rows, LANES), jnp.float32),
        ),
        in_specs=[hbm] * 4 + [pl.BlockSpec(memory_space=pltpu.SMEM)] + [hbm] * 4,
        out_specs=(vmem,) * 2,
        scratch_shapes=[
            pltpu.VMEM(features.shape, jnp.bfloat16),
            pltpu.VMEM((1, n_slot), jnp.int32),
            pltpu.VMEM((1, n_slot), jnp.int32),
            pltpu.VMEM((1, rows_dev), jnp.int32),
            pltpu.VMEM((F, HID), jnp.bfloat16),
            pltpu.VMEM((F, HID), jnp.bfloat16),
            pltpu.VMEM((C, HID), jnp.bfloat16),
            dma((7,)),
            pltpu.VMEM((CHUNKS, n_slot, tile_size // CHUNKS), jnp.bfloat16),
            pltpu.VMEM((dst_tiles * n_col * pairs, LANES), jnp.float32),
            pltpu.VMEM((2 * dst_tiles * pairs, n_col * LANES), jnp.bfloat16),
            pltpu.VMEM((n_row * 2 * rows_dev, F), jnp.bfloat16),
            pltpu.VMEM((rows_dev, F), jnp.float32),
            pltpu.VMEM((2, all_rows, LANES), jnp.float32),
            pltpu.VMEM((all_rows, LANES), jnp.float32),
            pltpu.VMEM((all_rows, LANES), jnp.float32),
            pltpu.VMEM((n_row, each, LANES), jnp.int16),
            pltpu.VMEM((peers, each, LANES), jnp.int16),
            pltpu.VMEM((n_row, each, LANES), jnp.int16),
            dma((CHUNKS,)), dma((peers,)), dma((peers,)), dma((peers,)), dma((peers,)),
            dma((3,)), dma((3,)), dma((peers,)), dma((peers,)), dma((peers,)), dma((peers,)),
        ],
        compiler_params=pltpu.CompilerParams(
            collective_id=0, has_side_effects=True, vmem_limit_bytes=60 * 2**20
        ),
    )(
        features, tile_values, tile_cols.reshape(1, n_slot), tile_rows.reshape(1, n_slot),
        tile_count, labels.reshape(1, rows_dev), w_self, w_neigh, w_out.T,
    )
    hidden, grad_self, grad_neigh, grad_out = pl.pallas_call(
        deliver,
        out_shape=(
            jax.ShapeDtypeStruct((rows_dev, HID), jnp.bfloat16),
            jax.ShapeDtypeStruct((F // 2, HID), jnp.float32),
            jax.ShapeDtypeStruct((F // 2, HID), jnp.float32),
            jax.ShapeDtypeStruct((C, HID // 2), jnp.float32),
        ),
        in_specs=[vmem] * 2,
        out_specs=(hbm,) * 4,
        scratch_shapes=[dma((6,))],
        compiler_params=pltpu.CompilerParams(vmem_limit_bytes=2**20),
    )(hidden, total)
    return hidden, grad_self, grad_neigh, grad_out.T


step_slots = 64


def aggregate(blocks_all, values, src_cols, dst_rows, live_count, rows_dev):
    slot_total = values.shape[0]
    dst_tiles = rows_dev // TB
    is_live = jnp.arange(slot_total) < live_count
    chosen = ((dst_rows[:, None] == jnp.arange(dst_tiles)[None, :]) & is_live[:, None]).astype(
        jnp.float32
    )
    turns = slot_total // step_slots
    tile_set = values.reshape(turns, step_slots, TB, TB)
    col_sets = src_cols.reshape(turns, step_slots)
    sel_sets = chosen.reshape(turns, step_slots, dst_tiles)

    def one_block(carry, pieces):
        tile_blk, col_blk, sel_blk = pieces
        gathered = blocks_all[col_blk]
        product = jnp.einsum("sij,sjf->sif", tile_blk, gathered, preferred_element_type=jnp.float32)
        total = carry[0] + jnp.einsum(
            "st,sif->tif", sel_blk, product, precision=lax.Precision.HIGHEST
        )
        row_sums = jnp.sum(tile_blk.astype(jnp.float32), axis=2)
        degree = carry[1] + jnp.einsum(
            "st,si->ti", sel_blk, row_sums, precision=lax.Precision.HIGHEST
        )
        return ((total, degree), None)

    start = (jnp.zeros((dst_tiles, TB, F), jnp.float32), jnp.zeros((dst_tiles, TB), jnp.float32))
    (total, degree), _ = lax.scan(one_block, start, (tile_set, col_sets, sel_sets))
    averaged = total / degree[:, :, None]
    return averaged.reshape(dst_tiles * TB, F).astype(jnp.bfloat16)


def local_wide(features, tile_values, tile_cols, tile_rows, tile_count, labels, w_self, w_neigh, w_out):
    rows_dev = labels.shape[0]
    n_row = lax.axis_size("row")
    n_rep = lax.axis_size("rep")
    rep_index = lax.axis_index("rep")
    own_rows = lax.dynamic_slice_in_dim(features, rep_index * rows_dev, rows_dev, 0)
    whole = lax.all_gather(features, "row", axis=0, tiled=True)
    blocks_all = whole.reshape(whole.shape[0] // TB, TB, F)
    neigh = aggregate(blocks_all, tile_values, tile_cols, tile_rows, tile_count[0], rows_dev)
    pre_act = jnp.dot(own_rows, w_self, preferred_element_type=jnp.float32) + jnp.dot(
        neigh, w_neigh, preferred_element_type=jnp.float32
    )
    hidden = jnp.maximum(pre_act, 0.0).astype(jnp.bfloat16)
    logits = jnp.dot(hidden, w_out, preferred_element_type=jnp.float32)
    row_max = jnp.max(logits, axis=1, keepdims=True)
    expo = jnp.exp(logits - row_max)
    probability = expo / jnp.sum(expo, axis=1, keepdims=True)
    one_hot = (labels[:, None] == jnp.arange(C)[None, :]).astype(jnp.float32)
    factor = 1.0 / math.sqrt(rows_dev * n_row * n_rep)
    d_logits = ((probability - one_hot) * factor).astype(jnp.bfloat16)
    part_out = jnp.dot(hidden.T, d_logits, preferred_element_type=jnp.float32)
    back = jnp.dot(d_logits, w_out.T, preferred_element_type=jnp.float32)
    d_pre = jnp.where(pre_act > 0.0, back, 0.0).astype(jnp.bfloat16)
    part_self = jnp.dot(own_rows.T, d_pre, preferred_element_type=jnp.float32)
    part_neigh = jnp.dot(neigh.T, d_pre, preferred_element_type=jnp.float32)
    summed = lax.psum((part_self, part_neigh, part_out), ("row", "rep"))
    feat_rows = F // n_rep
    hid_rows = HID // n_rep
    grad_self = lax.dynamic_slice_in_dim(summed[0], rep_index * feat_rows, feat_rows, 0)
    grad_neigh = lax.dynamic_slice_in_dim(summed[1], rep_index * feat_rows, feat_rows, 0)
    grad_out = lax.dynamic_slice_in_dim(summed[2], rep_index * hid_rows, hid_rows, 0)
    return (hidden, grad_self, grad_neigh, grad_out)


def solution(mesh):
    placed = (
        P(("parts", "row"), None),
        P(("parts", "row", "rep"), None),
        P(("parts", "row", "rep")),
        P(("parts", "row", "rep")),
        P(("parts", "row", "rep")),
        P(("parts", "row", "rep")),
        P(),
        P(),
        P(),
    )
    return jax.shard_map(
        local if mesh.shape["row"] in (2, 4, 8) else local_wide,
        mesh=mesh,
        in_specs=placed,
        out_specs=(
            P(("parts", "row", "rep"), None),
            P(("parts", "rep"), None),
            P(("parts", "rep"), None),
            P(("parts", "rep"), None),
        ),
        check_vma=False,
    )
```
